256 devices in a mesh: cd: 32 (over x, y, core), ab: 8 (over z).
Axes of the slice: x: 4, y: 4, z: 8, core: 2. Of those that a mesh axis runs over, the one named last changes fastest.
Arguments:
- amplitudes: float32 [1024, 65536], P('ab', 'cd'), may hold values from -6 to 6
- integrals: float32 [65536, 4096], P('cd', 'ab'), may hold values from -0.0234375 to 0.0234375
- live_tiles: int32 [256], P('cd'), may hold values from 0 to 1, as said below
- residual_in: float32 [1024, 4096], P(('ab', 'cd')), may hold values from -6 to 6
Outputs:
- residual_out: float32 [1024, 4096], P(('ab', 'cd'))
The draws below stay inside these ranges and needn't reach their ends.
Inputs may be any that keep to these rules, and one draw needn't show every extreme that they name: live_tiles[t] is 1 where tile t of 256 contracted pairs carries integrals and 0 where it is screened out; the 8 tiles of each index of cd hold at least one live tile.
All inputs are finite; a program needn't handle non-finite values.
Results may differ from the reference program's by a relative error of at most 0.0001.
Values sent between devices are 32-bit elements; how exact they have to be, the bound alone decides.
A program may use at most 128 MiB of HBM per device.

```python
import jax
import jax.numpy as jnp
from jax import lax

IJ = 1024
AB = 4096
TILE = 256
CD_DEV = 2048
TILES_DEV = 8
CD = 65536
N_CD = 32


def draw_live_tiles(key, part):
    key = jax.random.fold_in(key, 11)
    groups = CD // TILE // TILES_DEV
    count_key, order_key = jax.random.split(key)
    counts = jax.random.randint(count_key, (groups, 1), 1, TILES_DEV + 1)
    order_keys = jax.random.split(order_key, groups)
    orders = jax.vmap(lambda single: jax.random.permutation(single, TILES_DEV))(order_keys)
    return (orders < counts).astype(jnp.int32).reshape(-1)


def shard_levels(key, shape, cuts, least, high):
    def one(axis_at, shards_of):
        steps = jax.random.uniform(jax.random.fold_in(jax.random.fold_in(key, 6), axis_at), (shards_of,), jnp.float32, least / len(cuts), high / len(cuts))
        return jnp.repeat(jnp.exp(steps), shape[axis_at] // shards_of).reshape((-1,) + (1,) * (len(shape) - axis_at - 1))

    factor_of = one(*cuts[0])
    for cut in cuts[1:]:
        factor_of = factor_of * one(*cut)
    return factor_of


def centred(key, extent, deviation, bound, cuts=(), dtype=jnp.bfloat16):
    result = deviation * jax.random.normal(key, extent, jnp.float32)
    if cuts:
        result = result * shard_levels(key, extent, cuts, -0.22, 0.18)
    return jnp.clip(result, -bound, bound).astype(dtype)


def setup_inputs(seed: int = 0) -> dict:
    keys = jax.random.split(jax.random.key(seed), 5)
    amplitudes = centred(keys[0], (IJ, CD), 1.0, 6.0, ((0, 8), (1, 32)), jnp.float32)
    integrals = centred(keys[1], (CD, AB), CD ** -0.5, 0.0234375, ((0, 32), (1, 8)), jnp.float32)
    live_tiles = draw_live_tiles(jax.random.fold_in(keys[4], 71), 0)
    residual_in = centred(keys[3], (IJ, AB), 1.0, 6.0, ((0, 256),), jnp.float32)
    return {"amplitudes": amplitudes, "integrals": integrals, "live_tiles": live_tiles, "residual_in": residual_in}


def reference(amplitudes, integrals, live_tiles, residual_in):
    def add_block(block, total):
        first = (block * CD_DEV).astype(jnp.int32)
        left_part = lax.dynamic_slice_in_dim(amplitudes, first, CD_DEV, 1)
        right_part = lax.dynamic_slice_in_dim(integrals, first, CD_DEV, 0)
        flag_first = (block * TILES_DEV).astype(jnp.int32)
        flags = lax.dynamic_slice_in_dim(live_tiles, flag_first, TILES_DEV, 0)
        weights = jnp.repeat(flags.astype(jnp.float32), TILE, total_repeat_length=CD_DEV)
        return total + jnp.dot(left_part, right_part * weights[:, None], preferred_element_type=jnp.float32, precision=lax.Precision.HIGHEST)

    ladder = lax.fori_loop(jnp.int32(0), jnp.int32(N_CD), add_block, jnp.zeros((IJ, AB), jnp.float32))
    return residual_in + ladder
```

```python
import functools

import jax
import jax.numpy as jnp
from jax import lax
from jax.experimental import pallas as pl
from jax.experimental.pallas import tpu as pltpu
from jax.sharding import PartitionSpec as P

TILE = 256
HALF = 256
MESH = pl.DeviceIdType.MESH


def kernel(
    planes,
    chips,
    tiles,
    a_ref,
    b_ref,
    live_ref,
    residual_ref,
    out_ref,
    a_all,
    b_raw,
    b_hi,
    b_lo,
    part,
    pair_recv,
    plane_recv,
    summed,
    land,
    a_sem,
    b_sem,
    up_send,
    up_recv,
    down_send,
    down_recv,
    pair_send,
    pair_got,
    plane_send,
    plane_got,
    row_send,
    row_got,
):
    cd = lax.axis_index("cd")
    z = lax.axis_index("ab")
    chip, core = cd // 2, cd % 2
    twin = cd + 1 - 2 * core
    above, below = (z + 1) % planes, (z + planes - 1) % planes
    middle = planes // 2
    rows = a_ref.shape[0]

    barrier = pltpu.get_barrier_semaphore()

    def greet(cd_at, z_at):
        pl.semaphore_signal(barrier, inc=1, device_id={"cd": cd_at, "ab": z_at}, device_id_type=MESH)

    greet(cd, above)
    greet(cd, below)
    greet(twin, z)
    greet(twin, above)
    greet(twin, below)

    @pl.loop(2, planes - 1)
    def _(d):
        greet(cd, (z + d) % planes)
        greet(twin, (z + d) % planes)

    @pl.loop(1, chips)
    def _(d):
        greet(((chip + d) % chips) * 2 + core, z)

    def own_copy(t):
        return pltpu.make_async_copy(
            a_ref.at[:, pl.ds(pl.multiple_of(t * TILE, TILE), TILE)], a_all.at[0, t], a_sem.at[t]
        )

    def b_copy(t):
        return pltpu.make_async_copy(
            b_ref.at[pl.ds(pl.multiple_of(t * TILE, TILE), TILE), :], b_raw.at[t], b_sem.at[t]
        )

    @pl.loop(0, tiles)
    def _(t):
        own_copy(t).start()
        b_copy(t).start()

    part[...] = jnp.zeros_like(part)
    pl.semaphore_wait(barrier, 2 * (planes - 1) + chips)

    def up_copy(step, t):
        return pltpu.make_async_remote_copy(
            src_ref=a_all.at[step, t],
            dst_ref=a_all.at[step + 1, t],
            send_sem=up_send.at[step, t],
            recv_sem=up_recv.at[step, t],
            device_id={"cd": cd, "ab": above},
            device_id_type=MESH,
        )

    def down_copy(step, t):
        return pltpu.make_async_remote_copy(
            src_ref=a_all.at[(planes - step) % planes, t],
            dst_ref=a_all.at[planes - 1 - step, t],
            send_sem=down_send.at[step, t],
            recv_sem=down_recv.at[step, t],
            device_id={"cd": cd, "ab": below},
            device_id_type=MESH,
        )

    @pl.loop(0, tiles)
    def _(t):
        own_copy(t).wait()

    @pl.loop(0, tiles)
    def _(t):
        up_copy(0, t).start()
        down_copy(0, tiles - 1 - t).start()

    @pl.loop(0, tiles)
    def _(t):
        b_copy(t).wait()
        weight = live_ref[t].astype(jnp.float32)
        whole = b_raw[t] * weight
        high = whole.astype(jnp.bfloat16)
        b_hi[t] = high
        b_lo[t] = (whole - high.astype(jnp.float32)).astype(jnp.bfloat16)

    def multiply(slot, t):
        whole = a_all[slot, t]
        high = whole.astype(jnp.bfloat16)
        low = (whole - high.astype(jnp.float32)).astype(jnp.bfloat16)
        both = jnp.concatenate([high, low], axis=0)
        for h in range(2):
            cols = slice(h * HALF, (h + 1) * HALF)
            first = jnp.dot(both, b_hi[t, :, cols], preferred_element_type=jnp.float32)
            second = jnp.dot(high, b_lo[t, :, cols], preferred_element_type=jnp.float32)
            part[slot, h] += first[:rows] + (first[rows:] + second)

    def pair_copy(slot):
        return pltpu.make_async_remote_copy(
            src_ref=part.at[slot, 1 - core],
            dst_ref=pair_recv.at[slot],
            send_sem=pair_send.at[slot],
            recv_sem=pair_got.at[slot],
            device_id={"cd": twin, "ab": z},
            device_id_type=MESH,
        )

    def plane_copy(slot, d):
        to = (chip + d) % chips
        return pltpu.make_async_remote_copy(
            src_ref=part.at[slot, core, pl.ds(pl.multiple_of(to * 8, 8), 8)],
            dst_ref=plane_recv.at[slot, pl.ds(pl.multiple_of((d - 1) * 8, 8), 8)],
            send_sem=plane_send.at[slot],
            recv_sem=plane_got.at[slot],
            device_id={"cd": to * 2 + core, "ab": z},
            device_id_type=MESH,
        )

    def plane_whole(slot):
        return pltpu.make_async_remote_copy(
            src_ref=part.at[slot, core, pl.ds(0, (chips - 1) * 8)],
            dst_ref=plane_recv.at[slot],
            send_sem=plane_send.at[slot],
            recv_sem=plane_got.at[slot],
            device_id={"cd": twin, "ab": z},
            device_id_type=MESH,
        )

    def row_copy(slot, to_twin):
        return pltpu.make_async_remote_copy(
            src_ref=summed.at[slot],
            dst_ref=land.at[2 * z + core],
            send_sem=row_send.at[slot, to_twin],
            recv_sem=row_got.at[2 * z + core],
            device_id={"cd": twin if to_twin else cd, "ab": (z + planes - slot) % planes},
            device_id_type=MESH,
        )

    def send_pair(slot):
        pair_copy(slot).start()

    def send_plane(slot):
        pair_copy(slot).wait_recv()
        part[slot, core] += pair_recv[slot]

        @pl.loop(1, chips)
        def _(d):
            plane_copy(slot, d).start()

    def send_rows(slot):
        plane_whole(slot).wait_recv()
        mine = part[slot, core, pl.ds(pl.multiple_of(chip * 8, 8), 8)]
        total = mine + jnp.sum(plane_recv[slot].reshape(chips - 1, 8, HALF), axis=0)
        summed[slot] = total
        row_copy(slot, 1).start()
        if isinstance(slot, int) and slot == 0:
            land[2 * z + core] = total
        else:
            row_copy(slot, 0).start()

    @pl.loop(0, tiles)
    def _(t):
        multiply(0, t)

    send_pair(0)
    send_plane(0)

    def ring_step(step, j):
        up_copy(step - 1, j).wait_recv()

        @pl.when(jnp.logical_or(step < middle - 1, j < tiles // 2))
        def _():
            up_copy(step, j).start()

        down_copy(step - 1, tiles - 1 - j).wait_recv()

        @pl.when(jnp.logical_or(step < middle - 1, j < tiles // 2))
        def _():
            down_copy(step, tiles - 1 - j).start()

        multiply(step, j)
        multiply(planes - step, tiles - 1 - j)

    @pl.loop(1, middle)
    def _(step):
        @pl.loop(0, tiles)
        def _(j):
            ring_step(step, j)

            @pl.when(jnp.logical_and(step == 1, j == 2))
            def _():
                send_rows(0)

            @pl.when(jnp.logical_and(step > 1, j == 0))
            def _():
                send_plane(step - 1)
                send_plane(planes - step + 1)

            @pl.when(jnp.logical_and(step > 1, j == 3))
            def _():
                send_rows(step - 1)
                send_rows(planes - step + 1)

        send_pair(step)
        send_pair(planes - step)

    @pl.loop(0, tiles // 2)
    def _(j):
        up_copy(middle - 1, j).wait_recv()
        down_copy(middle - 1, tiles - 1 - j).wait_recv()
        multiply(middle, j)
        multiply(middle, tiles - 1 - j)

        @pl.when(j == 0)
        def _():
            send_plane(middle - 1)
            send_plane(middle + 1)

        @pl.when(j == tiles // 4)
        def _():
            send_rows(middle - 1)
            send_rows(middle + 1)

    send_pair(middle)
    send_plane(middle)
    send_rows(middle)

    @pl.loop(1, 2 * planes)
    def _(d):
        at = (2 * z + core + d) % (2 * planes)
        pltpu.make_async_remote_copy(
            src_ref=summed.at[0],
            dst_ref=land.at[at],
            send_sem=row_send.at[0, 0],
            recv_sem=row_got.at[at],
            device_id={"cd": twin, "ab": z},
            device_id_type=MESH,
        ).wait_recv()

    for at in range(2 * planes):
        cols = slice(at * HALF, (at + 1) * HALF)
        got = land[at]
        out_ref[:, cols] = residual_ref[:, cols] + jnp.where(core == 0, got[:4], got[4:])

    @pl.loop(0, middle)
    def _(step):
        @pl.loop(0, tiles)
        def _(j):
            @pl.when(jnp.logical_or(step < middle - 1, j < tiles // 2))
            def _():
                up_copy(step, j).wait_send()
                down_copy(step, tiles - 1 - j).wait_send()

    @pl.loop(0, planes)
    def _(slot):
        pair_copy(slot).wait_send()
        plane_whole(slot).wait_send()
        row_copy(slot, 1).wait_send()

        @pl.when(slot > 0)
        def _():
            row_copy(slot, 0).wait_send()


def solution(mesh):
    planes, chips = mesh.shape["ab"], mesh.shape["cd"] // 2

    def per_device(amplitudes, integrals, live_tiles, residual_in):
        rows, depth = amplitudes.shape
        tiles, columns = depth // TILE, integrals.shape[1]
        f32, bf16 = jnp.float32, jnp.bfloat16
        dma = pltpu.SemaphoreType.DMA
        return pl.pallas_call(
            functools.partial(kernel, planes, chips, tiles),
            out_shape=jax.ShapeDtypeStruct(residual_in.shape, f32),
            in_specs=[
                pl.BlockSpec(memory_space=pl.ANY),
                pl.BlockSpec(memory_space=pl.ANY),
                pl.BlockSpec(memory_space=pltpu.SMEM),
                pl.BlockSpec(memory_space=pltpu.VMEM),
            ],
            out_specs=pl.BlockSpec(memory_space=pltpu.VMEM),
            scratch_shapes=[
                pltpu.VMEM((planes, tiles, rows, TILE), f32),
                pltpu.VMEM((tiles, TILE, columns), f32),
                pltpu.VMEM((tiles, TILE, columns), bf16),
                pltpu.VMEM((tiles, TILE, columns), bf16),
                pltpu.VMEM((planes, 2, rows, HALF), f32),
                pltpu.VMEM((planes, rows, HALF), f32),
                pltpu.VMEM((planes, (chips - 1) * 8, HALF), f32),
                pltpu.VMEM((planes, 8, HALF), f32),
                pltpu.VMEM((2 * planes, 8, HALF), f32),
                dma((tiles,)),
                dma((tiles,)),
                dma((planes // 2, tiles)),
                dma((planes // 2, tiles)),
                dma((planes // 2, tiles)),
                dma((planes // 2, tiles)),
                dma((planes,)),
                dma((planes,)),
                dma((planes,)),
                dma((planes,)),
                dma((planes, 2)),
                dma((2 * planes,)),
            ],
            compiler_params=pltpu.CompilerParams(
                collective_id=0, has_side_effects=True, vmem_limit_bytes=48 * 1024 * 1024
            ),
            cost_estimate=pl.CostEstimate(
                flops=6 * planes * rows * depth * columns,
                bytes_accessed=4 * depth * (rows + columns),
                transcendentals=0,
            ),
        )(amplitudes, integrals, live_tiles, residual_in)

    return jax.shard_map(
        per_device,
        mesh=mesh,
        in_specs=(P("ab", "cd"), P("cd", "ab"), P("cd"), P(("ab", "cd"), None)),
        out_specs=P(("ab", "cd"), None),
        check_vma=False,
    )
```

```python
import functools

import jax
import jax.numpy as jnp
from jax import lax
from jax.experimental import pallas as pl
from jax.experimental.pallas import tpu as pltpu
from jax.sharding import PartitionSpec as P

TILE = 256
HALF = 256
MESH = pl.DeviceIdType.MESH


def kernel(
    planes,
    chips,
    tiles,
    a_ref,
    b_ref,
    live_ref,
    out_ref,
    a_all,
    b_raw,
    b_hi,
    b_lo,
    part,
    folded,
    pair_recv,
    plane_recv,
    summed,
    land,
    live,
    live_sem,
    a_sem,
    b_sem,
    up_send,
    up_recv,
    down_send,
    down_recv,
    pair_send,
    pair_got,
    plane_send,
    plane_got,
    row_send,
    row_got,
):
    cd = lax.axis_index("cd")
    z = lax.axis_index("ab")
    chip, core = cd // 2, cd % 2
    twin = cd + 1 - 2 * core
    above, below = (z + 1) % planes, (z + planes - 1) % planes
    middle = planes // 2
    rows = a_ref.shape[0]

    barrier = pltpu.get_barrier_semaphore()

    def greet(cd_at, z_at):
        pl.semaphore_signal(barrier, inc=1, device_id={"cd": cd_at, "ab": z_at}, device_id_type=MESH)

    greet(cd, above)
    greet(cd, below)
    greet(twin, z)

    @pl.loop(2, planes - 1)
    def _(d):
        greet(cd, (z + d) % planes)

    @pl.loop(1, chips)
    def _(d):
        greet(((chip + d) % chips) * 2 + core, z)

    def a_tile(t):
        return a_ref.at[:, pl.ds(pl.multiple_of(t * TILE, TILE), TILE)]

    def own_copy(t):
        return pltpu.make_async_copy(a_tile(t), a_all.at[0, t], a_sem.at[t])

    def b_copy(t):
        return pltpu.make_async_copy(
            b_ref.at[pl.ds(pl.multiple_of(t * TILE, TILE), TILE), :], b_raw.at[t], b_sem.at[t]
        )

    live_copy = pltpu.make_async_copy(live_ref, live, live_sem)
    live_copy.start()

    @pl.loop(0, tiles)
    def _(t):
        own_copy(t).start()
        b_copy(t).start()

    pl.semaphore_wait(barrier, planes - 1 + chips)

    def up_copy(step, t, src=None):
        return pltpu.make_async_remote_copy(
            src_ref=a_all.at[step, t] if src is None else src,
            dst_ref=a_all.at[step + 1, t],
            send_sem=up_send.at[step, t],
            recv_sem=up_recv.at[step, t],
            device_id={"cd": cd, "ab": above},
            device_id_type=MESH,
        )

    def down_copy(step, t, src=None):
        return pltpu.make_async_remote_copy(
            src_ref=a_all.at[(planes - step) % planes, t] if src is None else src,
            dst_ref=a_all.at[planes - 1 - step, t],
            send_sem=down_send.at[step, t],
            recv_sem=down_recv.at[step, t],
            device_id={"cd": cd, "ab": below},
            device_id_type=MESH,
        )

    @pl.loop(0, tiles)
    def _(t):
        up_copy(0, t, a_tile(t)).start()
        down_copy(0, tiles - 1 - t, a_tile(tiles - 1 - t)).start()

    part[...] = jnp.zeros_like(part)

    live_copy.wait()

    @pl.loop(0, tiles)
    def _(t):
        b_copy(t).wait()
        weight = live[t].astype(jnp.float32)
        whole = b_raw[t] * weight
        high = whole.astype(jnp.bfloat16)
        b_hi[t] = high
        b_lo[t] = (whole - high.astype(jnp.float32)).astype(jnp.bfloat16)

    def multiply(slot, t):
        whole = a_all[slot, t]
        high = whole.astype(jnp.bfloat16)
        low = (whole - high.astype(jnp.float32)).astype(jnp.bfloat16)
        both = jnp.concatenate([high, low], axis=0)
        for h in range(2):
            cols = slice(h * HALF, (h + 1) * HALF)
            first = jnp.dot(both, b_hi[t, :, cols], preferred_element_type=jnp.float32)
            second = jnp.dot(high, b_lo[t, :, cols], preferred_element_type=jnp.float32)
            part[slot, h] += first[:rows] + (first[rows:] + second)

    def pair_copy(slot):
        return pltpu.make_async_remote_copy(
            src_ref=folded.at[slot, 1 - core],
            dst_ref=pair_recv.at[slot],
            send_sem=pair_send.at[slot],
            recv_sem=pair_got.at[slot],
            device_id={"cd": twin, "ab": z},
            device_id_type=MESH,
        )

    def plane_copy(slot, d):
        to = (chip + d) % chips
        return pltpu.make_async_remote_copy(
            src_ref=folded.at[slot, core, pl.ds(pl.multiple_of(to * 8, 8), 8)],
            dst_ref=plane_recv.at[slot, pl.ds(pl.multiple_of((d - 1) * 8, 8), 8)],
            send_sem=plane_send.at[slot],
            recv_sem=plane_got.at[slot],
            device_id={"cd": to * 2 + core, "ab": z},
            device_id_type=MESH,
        )

    def plane_whole(slot):
        return pltpu.make_async_remote_copy(
            src_ref=folded.at[slot, core, pl.ds(0, (chips - 1) * 8)],
            dst_ref=plane_recv.at[slot],
            send_sem=plane_send.at[slot],
            recv_sem=plane_got.at[slot],
            device_id={"cd": twin, "ab": z},
            device_id_type=MESH,
        )

    def row_copy(slot):
        return pltpu.make_async_remote_copy(
            src_ref=summed.at[slot],
            dst_ref=land.at[slot],
            send_sem=row_send.at[slot],
            recv_sem=row_got.at[slot],
            device_id={"cd": cd, "ab": (z + planes - slot) % planes},
            device_id_type=MESH,
        )

    def send_pair(slot):
        left, right = part[slot, 0], part[slot, 1]
        upper = lax.broadcasted_iota(jnp.int32, left.shape, 0) % 8 < 4
        folded[slot, 0] = jnp.where(upper, left, pltpu.roll(right, 4, 0))
        folded[slot, 1] = jnp.where(upper, pltpu.roll(left, rows - 4, 0), right)
        pair_copy(slot).start()

    def send_plane(slot):
        pair_copy(slot).wait_recv()
        folded[slot, core] += pair_recv[slot]

        @pl.loop(1, chips)
        def _(d):
            plane_copy(slot, d).start()

    def write_rows(slot, got):
        first = ((z + slot) % planes) * (2 * HALF)
        for h in range(2):
            cols = pl.ds(pl.multiple_of(first + h * HALF, HALF), HALF)
            out_ref[:, cols] = got[4 * h : 4 * h + 4]

    def send_rows(slot):
        plane_whole(slot).wait_recv()
        mine = folded[slot, core, pl.ds(pl.multiple_of(chip * 8, 8), 8)]
        total = mine + jnp.sum(plane_recv[slot].reshape(chips - 1, 8, HALF), axis=0)
        if isinstance(slot, int) and slot == 0:
            write_rows(0, total)
        else:
            summed[slot] = total

    def take_rows(slot):
        row_copy(slot).wait_recv()
        write_rows(slot, land[slot])

    def ring_sent(step, j):
        up_copy(step, j).wait_send()
        down_copy(step, tiles - 1 - j).wait_send()

    @pl.loop(0, tiles)
    def _(t):
        own_copy(t).wait()
        multiply(0, t)

    send_pair(0)
    send_plane(0)

    def ring_step(step, j):
        up_copy(step - 1, j).wait_recv()

        @pl.when(jnp.logical_or(step < middle - 1, j < tiles // 2))
        def _():
            up_copy(step, j).start()

        down_copy(step - 1, tiles - 1 - j).wait_recv()

        @pl.when(jnp.logical_or(step < middle - 1, j < tiles // 2))
        def _():
            down_copy(step, tiles - 1 - j).start()

        multiply(step, j)
        multiply(planes - step, tiles - 1 - j)

        @pl.when(step > 1)
        def _():
            ring_sent(step - 2, j)

    @pl.loop(1, middle)
    def _(step):
        @pl.loop(0, tiles)
        def _(j):
            ring_step(step, j)

            @pl.when(jnp.logical_and(step == 1, j == 2))
            def _():
                send_rows(0)

            @pl.when(jnp.logical_and(step > 1, j == 0))
            def _():
                send_plane(step - 1)
                send_plane(planes - step + 1)

            @pl.when(jnp.logical_and(step > 1, j == 3))
            def _():
                send_rows(step - 1)
                send_rows(planes - step + 1)

        send_pair(step)
        send_pair(planes - step)

    @pl.loop(0, tiles // 2)
    def _(j):
        up_copy(middle - 1, j).wait_recv()
        down_copy(middle - 1, tiles - 1 - j).wait_recv()
        multiply(middle, j)
        multiply(middle, tiles - 1 - j)

        @pl.when(j == 0)
        def _():
            send_plane(middle - 1)
            send_plane(middle + 1)

        @pl.when(j == tiles // 4)
        def _():
            send_rows(middle - 1)
            send_rows(middle + 1)

    send_pair(middle)

    @pl.loop(1, middle)
    def _(slot):
        row_copy(slot).start()
        row_copy(planes - slot).start()

    send_plane(middle)

    @pl.loop(0, tiles)
    def _(j):
        ring_sent(middle - 2, j)

    @pl.loop(0, tiles // 2)
    def _(j):
        ring_sent(middle - 1, j)

    send_rows(middle)
    row_copy(middle).start()

    @pl.loop(1, middle)
    def _(slot):
        take_rows(slot)
        take_rows(planes - slot)

    @pl.loop(0, planes)
    def _(slot):
        pair_copy(slot).wait_send()
        plane_whole(slot).wait_send()

        @pl.when(jnp.logical_and(slot > 0, slot != middle))
        def _():
            row_copy(slot).wait_send()

    take_rows(middle)
    row_copy(middle).wait_send()


def solution(mesh):
    planes, chips = mesh.shape["ab"], mesh.shape["cd"] // 2

    def per_device(amplitudes, integrals, live_tiles, residual_in):
        rows, depth = amplitudes.shape
        tiles, columns = depth // TILE, integrals.shape[1]
        f32, bf16 = jnp.float32, jnp.bfloat16
        dma = pltpu.SemaphoreType.DMA
        ladder = pl.pallas_call(
            functools.partial(kernel, planes, chips, tiles),
            out_shape=pltpu.VMEM(residual_in.shape, f32),
            in_specs=[
                pl.BlockSpec(memory_space=pltpu.HBM),
                pl.BlockSpec(memory_space=pltpu.HBM),
                pl.BlockSpec(memory_space=pltpu.HBM),
            ],
            out_specs=pl.BlockSpec(memory_space=pltpu.VMEM),
            scratch_shapes=[
                pltpu.VMEM((planes, tiles, rows, TILE), f32),
                pltpu.VMEM((tiles, TILE, columns), f32),
                pltpu.VMEM((tiles, TILE, columns), bf16),
                pltpu.VMEM((tiles, TILE, columns), bf16),
                pltpu.VMEM((planes, 2, rows, HALF), f32),
                pltpu.VMEM((planes, 2, rows, HALF), f32),
                pltpu.VMEM((planes, rows, HALF), f32),
                pltpu.VMEM((planes, (chips - 1) * 8, HALF), f32),
                pltpu.VMEM((planes, 8, HALF), f32),
                pltpu.VMEM((planes, 8, HALF), f32),
                pltpu.SMEM((tiles,), jnp.int32),
                dma(()),
                dma((tiles,)),
                dma((tiles,)),
                dma((planes // 2, tiles)),
                dma((planes // 2, tiles)),
                dma((planes // 2, tiles)),
                dma((planes // 2, tiles)),
                dma((planes,)),
                dma((planes,)),
                dma((planes,)),
                dma((planes,)),
                dma((planes,)),
                dma((planes,)),
            ],
            compiler_params=pltpu.CompilerParams(
                collective_id=0, has_side_effects=True, vmem_limit_bytes=58 * 1024 * 1024
            ),
            cost_estimate=pl.CostEstimate(
                flops=6 * planes * rows * depth * columns,
                bytes_accessed=4 * depth * (rows + columns),
                transcendentals=0,
            ),
        )(amplitudes, integrals, live_tiles)
        return residual_in + ladder

    return jax.shard_map(
        per_device,
        mesh=mesh,
        in_specs=(P("ab", "cd"), P("cd", "ab"), P("cd"), P(("ab", "cd"), None)),
        out_specs=P(("ab", "cd"), None),
        check_vma=False,
    )
```

```python
import functools
import math

import jax
import jax.numpy as jnp
from jax import lax
from jax.experimental import pallas as pl
from jax.experimental.pallas import tpu as pltpu
from jax.sharding import PartitionSpec as P

TILE = 256
HALF = 256
MESH = pl.DeviceIdType.MESH


def kernel(
    planes,
    chips,
    line,
    tiles,
    a_ref,
    b_ref,
    live_ref,
    out_ref,
    a_all,
    b_raw,
    b_hi,
    b_lo,
    part,
    folded,
    pair_recv,
    plane_recv,
    summed,
    land,
    live,
    relay,
    live_sem,
    a_sem,
    b_sem,
    up_send,
    up_recv,
    down_send,
    down_recv,
    pair_send,
    pair_got,
    plane_send,
    plane_got,
    row_send,
    row_got,
):
    cd = lax.axis_index("cd")
    z = lax.axis_index("ab")
    chip, core = cd // 2, cd % 2
    twin = cd + 1 - 2 * core
    above, below = (z + 1) % planes, (z + planes - 1) % planes
    half = tiles // 2
    last = planes - 1
    rows = a_ref.shape[0]

    barrier = pltpu.get_barrier_semaphore()

    def greet(cd_at, z_at):
        pl.semaphore_signal(barrier, inc=1, device_id={"cd": cd_at, "ab": z_at}, device_id_type=MESH)

    greet(cd, above)
    greet(cd, below)
    greet(twin, z)

    across, along = chip // line, chip % line

    def in_row(d):
        return (across * line + (along + d) % line) * 2 + core

    def in_column(d):
        return ((across + d) % line * line + along) * 2 + core

    @pl.loop(1, line)
    def _(d):
        greet(in_row(d), z)
        greet(in_column(d), z)

    def a_tile(t):
        return a_ref.at[:, pl.ds(pl.multiple_of(t * TILE, TILE), TILE)]

    def own_copy(t):
        return pltpu.make_async_copy(a_tile(t), a_all.at[0, t], a_sem.at[t])

    def b_copy(t):
        return pltpu.make_async_copy(
            b_ref.at[pl.ds(pl.multiple_of(t * TILE, TILE), TILE), :], b_raw.at[t], b_sem.at[t]
        )

    pl.semaphore_wait(barrier, 3 + 2 * (line - 1))

    def up_copy(step, t, src=None):
        return pltpu.make_async_remote_copy(
            src_ref=a_all.at[step, t] if src is None else src,
            dst_ref=a_all.at[step + 1, t],
            send_sem=up_send.at[step, t],
            recv_sem=up_recv.at[step, t],
            device_id={"cd": cd, "ab": above},
            device_id_type=MESH,
        )

    def down_copy(step, t, src=None):
        return pltpu.make_async_remote_copy(
            src_ref=a_all.at[(planes - step) % planes, t] if src is None else src,
            dst_ref=a_all.at[planes - 1 - step, t],
            send_sem=down_send.at[step, t],
            recv_sem=down_recv.at[step, t],
            device_id={"cd": cd, "ab": below},
            device_id_type=MESH,
        )

    @pl.loop(0, half)
    def _(t):
        up_copy(0, t, a_tile(t)).start()
        down_copy(0, tiles - 1 - t, a_tile(tiles - 1 - t)).start()

    up_copy(0, half, a_tile(half)).start()

    @pl.loop(1, line)
    def _(d):
        pl.semaphore_signal(relay, inc=1, device_id={"cd": in_row(d), "ab": z}, device_id_type=MESH)

    live_copy = pltpu.make_async_copy(live_ref, live, live_sem)
    live_copy.start()

    @pl.loop(0, tiles)
    def _(t):
        own_copy(t).start()
        b_copy(t).start()

    part[...] = jnp.zeros_like(part)

    live_copy.wait()

    @pl.loop(0, tiles)
    def _(t):
        b_copy(t).wait()
        weight = live[t].astype(jnp.float32)
        whole = b_raw[t] * weight
        high = whole.astype(jnp.bfloat16)
        b_hi[t] = high
        b_lo[t] = (whole - high.astype(jnp.float32)).astype(jnp.bfloat16)

    def multiply(slot, t):
        whole = a_all[slot, t]
        high = whole.astype(jnp.bfloat16)
        low = (whole - high.astype(jnp.float32)).astype(jnp.bfloat16)
        both = jnp.concatenate([high, low], axis=0)
        for h in range(2):
            cols = slice(h * HALF, (h + 1) * HALF)
            first = jnp.dot(both, b_hi[t, :, cols], preferred_element_type=jnp.float32)
            second = jnp.dot(high, b_lo[t, :, cols], preferred_element_type=jnp.float32)
            part[slot, h] += first[:rows] + (first[rows:] + second)

    def pair_copy(slot):
        return pltpu.make_async_remote_copy(
            src_ref=folded.at[slot, 1 - core],
            dst_ref=pair_recv.at[slot],
            send_sem=pair_send.at[slot],
            recv_sem=pair_got.at[slot],
            device_id={"cd": twin, "ab": z},
            device_id_type=MESH,
        )

    def plane_copy(slot, d):
        to = (chip + d) % chips
        return pltpu.make_async_remote_copy(
            src_ref=folded.at[slot, core, pl.ds(pl.multiple_of(to * 8, 8), 8)],
            dst_ref=plane_recv.at[slot, pl.ds(pl.multiple_of((d - 1) * 8, 8), 8)],
            send_sem=plane_send.at[slot],
            recv_sem=plane_got.at[slot],
            device_id={"cd": to * 2 + core, "ab": z},
            device_id_type=MESH,
        )

    def plane_whole(slot):
        return pltpu.make_async_remote_copy(
            src_ref=folded.at[slot, core, pl.ds(0, (chips - 1) * 8)],
            dst_ref=plane_recv.at[slot],
            send_sem=plane_send.at[slot],
            recv_sem=plane_got.at[slot],
            device_id={"cd": twin, "ab": z},
            device_id_type=MESH,
        )

    def row_copy(slot):
        return pltpu.make_async_remote_copy(
            src_ref=summed.at[slot],
            dst_ref=land.at[slot],
            send_sem=row_send.at[slot],
            recv_sem=row_got.at[slot],
            device_id={"cd": cd, "ab": (z + planes - slot) % planes},
            device_id_type=MESH,
        )

    def send_pair(slot):
        left, right = part[slot, 0], part[slot, 1]
        upper = lax.broadcasted_iota(jnp.int32, left.shape, 0) % 8 < 4
        folded[slot, 0] = jnp.where(upper, left, pltpu.roll(right, 4, 0))
        folded[slot, 1] = jnp.where(upper, pltpu.roll(left, rows - 4, 0), right)
        pair_copy(slot).start()

    def send_plane(slot):
        pair_copy(slot).wait_recv()
        folded[slot, core] += pair_recv[slot]

        @pl.loop(1, chips)
        def _(d):
            plane_copy(slot, d).start()

    def write_rows(slot, got):
        first = ((z + slot) % planes) * (2 * HALF)
        for h in range(2):
            cols = pl.ds(pl.multiple_of(first + h * HALF, HALF), HALF)
            out_ref[:, cols] = got[4 * h : 4 * h + 4]

    def send_rows(slot):
        plane_whole(slot).wait_recv()
        mine = folded[slot, core, pl.ds(pl.multiple_of(chip * 8, 8), 8)]
        total = mine + jnp.sum(plane_recv[slot].reshape(chips - 1, 8, HALF), axis=0)
        if isinstance(slot, int) and slot == 0:
            write_rows(0, total)
        else:
            summed[slot] = total

    def take_rows(slot):
        row_copy(slot).wait_recv()
        write_rows(slot, land[slot])

    @pl.loop(0, tiles)
    def _(t):
        own_copy(t).wait()

    def forward_up(step, j):
        up_copy(step - 1, j).wait_recv()

        @pl.when(jnp.logical_or(step < last - 1, jnp.logical_and(step < last, j < half - 1)))
        def _():
            up_copy(step, j).start()

    def forward_down(step, j):
        down_copy(step - 1, tiles - 1 - j).wait_recv()

        @pl.when(jnp.logical_or(step < last - 1, jnp.logical_and(step < last, j < half - 1)))
        def _():
            down_copy(step, tiles - 1 - j).start()

    def ring_sent(step, j):
        up_copy(step, j).wait_send()
        down_copy(step, tiles - 1 - j).wait_send()

    def plane_sent(slot):
        pair_copy(slot).wait_send()
        plane_whole(slot).wait_send()

    @pl.loop(1, last)
    def _(step):
        @pl.loop(0, half)
        def _(j):
            forward_up(step, j)
            forward_down(step, j)
            multiply(step, j)
            multiply(planes - step, tiles - 1 - j)

            @pl.when(step == 1)
            def _():
                multiply(0, j)
                multiply(0, tiles - 1 - j)

            @pl.when(step > 1)
            def _():
                ring_sent(step - 2, j)

            @pl.when(jnp.logical_and(step == 1, j == 2))
            def _():
                up_copy(0, half).wait_recv()
                multiply(1, half)

            @pl.when(jnp.logical_and(step == 2, j == 0))
            def _():
                pl.semaphore_wait(relay, line - 1)
                send_plane(0)

            @pl.when(jnp.logical_and(step == 2, j == 2))
            def _():
                send_rows(0)
                plane_sent(0)

            @pl.when(jnp.logical_and(step == planes // 2 + 1, j == 0))
            def _():
                send_plane(planes // 2)

            @pl.when(jnp.logical_and(step == planes // 2 + 1, j == 2))
            def _():
                send_rows(planes // 2)
                plane_sent(planes // 2)

            @pl.when(jnp.logical_and(step > planes // 2 + 1, j == 0))
            def _():
                send_plane(step - 1)
                send_plane(planes - step + 1)

            @pl.when(jnp.logical_and(step > planes // 2 + 1, j == 2))
            def _():
                send_rows(step - 1)
                send_rows(planes - step + 1)
                plane_sent(step - 1)
                plane_sent(planes - step + 1)

        @pl.when(step == 1)
        def _():
            send_pair(0)

        @pl.when(step == planes // 2)
        def _():
            send_pair(planes // 2)

        @pl.when(step > planes // 2)
        def _():
            send_pair(step)
            send_pair(planes - step)

    down_copy(0, half - 1, a_tile(half - 1)).start()

    @pl.loop(0, half - 1)
    def _(j):
        down_copy(last - 1, tiles - 1 - j).wait_recv()
        multiply(1, tiles - 1 - j)

        @pl.when(j > 0)
        def _():
            up_copy(last - 1, j - 1).wait_recv()
            multiply(last, j - 1)

        @pl.when(j == 0)
        def _():
            send_plane(last - 1)
            send_plane(2)

        @pl.when(j == half - 2)
        def _():
            send_pair(1)

    send_rows(last - 1)
    send_rows(2)
    plane_sent(last - 1)
    plane_sent(2)
    send_plane(1)
    up_copy(last - 1, half - 2).wait_recv()
    multiply(last, half - 2)
    down_copy(0, half - 1).wait_recv()
    multiply(last, half - 1)
    send_pair(last)

    @pl.loop(2, last)
    def _(slot):
        row_copy(slot).start()

    send_plane(last)
    send_rows(1)
    row_copy(1).start()

    @pl.loop(0, half)
    def _(j):
        ring_sent(last - 2, j)

    send_rows(last)
    row_copy(last).start()

    @pl.loop(0, half - 1)
    def _(j):
        ring_sent(last - 1, j)

    up_copy(0, half).wait_send()
    down_copy(0, half - 1).wait_send()
    plane_sent(1)
    plane_sent(last)

    @pl.loop(1, last)
    def _(slot):
        take_rows(slot)
        row_copy(slot).wait_send()

    take_rows(last)
    row_copy(last).wait_send()


def solution(mesh):
    planes, chips = mesh.shape["ab"], mesh.shape["cd"] // 2

    def per_device(amplitudes, integrals, live_tiles, residual_in):
        rows, depth = amplitudes.shape
        tiles, columns = depth // TILE, integrals.shape[1]
        f32, bf16 = jnp.float32, jnp.bfloat16
        dma = pltpu.SemaphoreType.DMA
        ladder = pl.pallas_call(
            functools.partial(kernel, planes, chips, math.isqrt(chips), tiles),
            out_shape=pltpu.VMEM(residual_in.shape, f32),
            in_specs=[
                pl.BlockSpec(memory_space=pltpu.HBM),
                pl.BlockSpec(memory_space=pltpu.HBM),
                pl.BlockSpec(memory_space=pltpu.HBM),
            ],
            out_specs=pl.BlockSpec(memory_space=pltpu.VMEM),
            scratch_shapes=[
                pltpu.VMEM((planes, tiles, rows, TILE), f32),
                pltpu.VMEM((tiles, TILE, columns), f32),
                pltpu.VMEM((tiles, TILE, columns), bf16),
                pltpu.VMEM((tiles, TILE, columns), bf16),
                pltpu.VMEM((planes, 2, rows, HALF), f32),
                pltpu.VMEM((planes, 2, rows, HALF), f32),
                pltpu.VMEM((planes, rows, HALF), f32),
                pltpu.VMEM((planes, (chips - 1) * 8, HALF), f32),
                pltpu.VMEM((planes, 8, HALF), f32),
                pltpu.VMEM((planes, 8, HALF), f32),
                pltpu.SMEM((tiles,), jnp.int32),
                pltpu.SemaphoreType.REGULAR,
                dma(()),
                dma((tiles,)),
                dma((tiles,)),
                dma((planes - 1, tiles)),
                dma((planes - 1, tiles)),
                dma((planes - 1, tiles)),
                dma((planes - 1, tiles)),
                dma((planes,)),
                dma((planes,)),
                dma((planes,)),
                dma((planes,)),
                dma((planes,)),
                dma((planes,)),
            ],
            compiler_params=pltpu.CompilerParams(
                collective_id=0, has_side_effects=True, vmem_limit_bytes=58 * 1024 * 1024
            ),
            cost_estimate=pl.CostEstimate(
                flops=6 * planes * rows * depth * columns,
                bytes_accessed=4 * depth * (rows + columns),
                transcendentals=0,
            ),
        )(amplitudes, integrals, live_tiles)
        return residual_in + ladder

    return jax.shard_map(
        per_device,
        mesh=mesh,
        in_specs=(P("ab", "cd"), P("cd", "ab"), P("cd"), P(("ab", "cd"), None)),
        out_specs=P(("ab", "cd"), None),
        check_vma=False,
    )
```

```python
import functools
import math

import jax
import jax.numpy as jnp
from jax import lax
from jax.experimental import pallas as pl
from jax.experimental.pallas import tpu as pltpu
from jax.sharding import PartitionSpec as P

TILE = 256
HALF = 256
MESH = pl.DeviceIdType.MESH


def kernel(
    planes,
    chips,
    line,
    tiles,
    a_ref,
    b_ref,
    live_ref,
    out_ref,
    a_all,
    b_raw,
    b_hi,
    b_lo,
    part,
    folded,
    pair_recv,
    plane_recv,
    summed,
    land,
    direct,
    live,
    relay,
    live_sem,
    a_sem,
    b_sem,
    up_send,
    up_recv,
    down_send,
    down_recv,
    pair_send,
    pair_got,
    plane_send,
    plane_got,
    row_send,
    row_got,
    direct_send,
    direct_got,
):
    cd = lax.axis_index("cd")
    z = lax.axis_index("ab")
    chip, core = cd // 2, cd % 2
    twin = cd + 1 - 2 * core
    above, below = (z + 1) % planes, (z + planes - 1) % planes
    half = tiles // 2
    last = planes - 1
    rows = a_ref.shape[0]

    barrier = pltpu.get_barrier_semaphore()

    def greet(cd_at, z_at):
        pl.semaphore_signal(barrier, inc=1, device_id={"cd": cd_at, "ab": z_at}, device_id_type=MESH)

    greet(cd, above)
    greet(cd, below)
    greet(twin, z)

    across, along = chip // line, chip % line

    def in_row(d):
        return (across * line + (along + d) % line) * 2 + core

    def in_column(d):
        return ((across + d) % line * line + along) * 2 + core

    @pl.loop(1, line)
    def _(d):
        greet(in_row(d), z)
        greet(in_column(d), z)

    def a_tile(t):
        return a_ref.at[:, pl.ds(pl.multiple_of(t * TILE, TILE), TILE)]

    def own_copy(t):
        return pltpu.make_async_copy(a_tile(t), a_all.at[0, t], a_sem.at[t])

    def b_copy(t):
        return pltpu.make_async_copy(
            b_ref.at[pl.ds(pl.multiple_of(t * TILE, TILE), TILE), :], b_raw.at[t], b_sem.at[t]
        )

    pl.semaphore_wait(barrier, 3 + 2 * (line - 1))

    def up_copy(step, t, src=None):
        return pltpu.make_async_remote_copy(
            src_ref=a_all.at[step, t] if src is None else src,
            dst_ref=a_all.at[step + 1, t],
            send_sem=up_send.at[step, t],
            recv_sem=up_recv.at[step, t],
            device_id={"cd": cd, "ab": above},
            device_id_type=MESH,
        )

    def down_copy(step, t, src=None):
        return pltpu.make_async_remote_copy(
            src_ref=a_all.at[(planes - step) % planes, t] if src is None else src,
            dst_ref=a_all.at[planes - 1 - step, t],
            send_sem=down_send.at[step, t],
            recv_sem=down_recv.at[step, t],
            device_id={"cd": cd, "ab": below},
            device_id_type=MESH,
        )

    @pl.loop(0, half)
    def _(t):
        up_copy(0, t, a_tile(t)).start()
        down_copy(0, tiles - 1 - t, a_tile(tiles - 1 - t)).start()

    up_copy(0, half, a_tile(half)).start()

    @pl.loop(1, line)
    def _(d):
        pl.semaphore_signal(relay, inc=1, device_id={"cd": in_row(d), "ab": z}, device_id_type=MESH)

    live_copy = pltpu.make_async_copy(live_ref, live, live_sem)
    live_copy.start()

    @pl.loop(0, tiles)
    def _(t):
        own_copy(t).start()
        b_copy(t).start()

    part[...] = jnp.zeros_like(part)

    live_copy.wait()

    @pl.loop(0, tiles)
    def _(t):
        b_copy(t).wait()
        weight = live[t].astype(jnp.float32)
        whole = b_raw[t] * weight
        high = whole.astype(jnp.bfloat16)
        b_hi[t] = high
        b_lo[t] = (whole - high.astype(jnp.float32)).astype(jnp.bfloat16)

    def multiply(slot, t):
        whole = a_all[slot, t]
        high = whole.astype(jnp.bfloat16)
        low = (whole - high.astype(jnp.float32)).astype(jnp.bfloat16)
        both = jnp.concatenate([high, low], axis=0)
        for h in range(2):
            cols = slice(h * HALF, (h + 1) * HALF)
            first = jnp.dot(both, b_hi[t, :, cols], preferred_element_type=jnp.float32)
            second = jnp.dot(high, b_lo[t, :, cols], preferred_element_type=jnp.float32)
            part[slot, h] += first[:rows] + (first[rows:] + second)

    def pair_copy(slot):
        return pltpu.make_async_remote_copy(
            src_ref=folded.at[slot, 1 - core],
            dst_ref=pair_recv.at[slot],
            send_sem=pair_send.at[slot],
            recv_sem=pair_got.at[slot],
            device_id={"cd": twin, "ab": z},
            device_id_type=MESH,
        )

    def plane_copy(slot, d):
        to = (chip + d) % chips
        return pltpu.make_async_remote_copy(
            src_ref=folded.at[slot, core, pl.ds(pl.multiple_of(to * 8, 8), 8)],
            dst_ref=plane_recv.at[slot, pl.ds(pl.multiple_of((d - 1) * 8, 8), 8)],
            send_sem=plane_send.at[slot],
            recv_sem=plane_got.at[slot],
            device_id={"cd": to * 2 + core, "ab": z},
            device_id_type=MESH,
        )

    def plane_whole(slot):
        return pltpu.make_async_remote_copy(
            src_ref=folded.at[slot, core, pl.ds(0, (chips - 1) * 8)],
            dst_ref=plane_recv.at[slot],
            send_sem=plane_send.at[slot],
            recv_sem=plane_got.at[slot],
            device_id={"cd": twin, "ab": z},
            device_id_type=MESH,
        )

    def row_copy(slot):
        return pltpu.make_async_remote_copy(
            src_ref=summed.at[slot],
            dst_ref=land.at[slot],
            send_sem=row_send.at[slot],
            recv_sem=row_got.at[slot],
            device_id={"cd": cd, "ab": (z + planes - slot) % planes},
            device_id_type=MESH,
        )

    away = sorted(
        ((dx, dy) for dx in range(line) for dy in range(line)),
        key=lambda d: -min(d[0], line - d[0]) - min(d[1], line - d[1]),
    )

    def direct_copy(at):
        dx, dy = away[at]
        to = (across + dx) % line * line + (along + dy) % line
        return pltpu.make_async_remote_copy(
            src_ref=folded.at[last, core, pl.ds(pl.multiple_of(to * 8, 8), 8)],
            dst_ref=direct.at[pl.ds(at * 8, 8)],
            send_sem=direct_send,
            recv_sem=direct_got,
            device_id={"cd": to * 2 + core, "ab": above},
            device_id_type=MESH,
        )

    def direct_whole():
        return pltpu.make_async_remote_copy(
            src_ref=folded.at[last, core],
            dst_ref=direct,
            send_sem=direct_send,
            recv_sem=direct_got,
            device_id={"cd": cd, "ab": above},
            device_id_type=MESH,
        )

    def send_direct():
        pair_copy(last).wait_recv()
        folded[last, core] += pair_recv[last]
        for at in range(chips):
            direct_copy(at).start()

    def take_direct():
        direct_whole().wait_recv()
        write_rows(last, jnp.sum(direct[...].reshape(chips, 8, HALF), axis=0))

    def send_pair(slot):
        left, right = part[slot, 0], part[slot, 1]
        upper = lax.broadcasted_iota(jnp.int32, left.shape, 0) % 8 < 4
        folded[slot, 0] = jnp.where(upper, left, pltpu.roll(right, 4, 0))
        folded[slot, 1] = jnp.where(upper, pltpu.roll(left, rows - 4, 0), right)
        pair_copy(slot).start()

    def send_plane(slot):
        pair_copy(slot).wait_recv()
        folded[slot, core] += pair_recv[slot]

        @pl.loop(1, chips)
        def _(d):
            plane_copy(slot, d).start()

    def write_rows(slot, got):
        first = ((z + slot) % planes) * (2 * HALF)
        for h in range(2):
            cols = pl.ds(pl.multiple_of(first + h * HALF, HALF), HALF)
            out_ref[:, cols] = got[4 * h : 4 * h + 4]

    def send_rows(slot):
        plane_whole(slot).wait_recv()
        mine = folded[slot, core, pl.ds(pl.multiple_of(chip * 8, 8), 8)]
        total = mine + jnp.sum(plane_recv[slot].reshape(chips - 1, 8, HALF), axis=0)
        if isinstance(slot, int) and slot == 0:
            write_rows(0, total)
        else:
            summed[slot] = total

    def take_rows(slot):
        row_copy(slot).wait_recv()
        write_rows(slot, land[slot])

    @pl.loop(0, tiles)
    def _(t):
        own_copy(t).wait()

    def forward_up(step, j):
        up_copy(step - 1, j).wait_recv()

        @pl.when(jnp.logical_or(step < last - 1, jnp.logical_and(step < last, j < half - 1)))
        def _():
            up_copy(step, j).start()

    def forward_down(step, j):
        down_copy(step - 1, tiles - 1 - j).wait_recv()

        @pl.when(jnp.logical_or(step < last - 1, jnp.logical_and(step < last, j < half - 1)))
        def _():
            down_copy(step, tiles - 1 - j).start()

    def ring_sent(step, j):
        up_copy(step, j).wait_send()
        down_copy(step, tiles - 1 - j).wait_send()

    def plane_sent(slot):
        pair_copy(slot).wait_send()
        plane_whole(slot).wait_send()

    @pl.loop(1, last)
    def _(step):
        @pl.loop(0, half)
        def _(j):
            forward_up(step, j)
            forward_down(step, j)
            multiply(step, j)
            multiply(planes - step, tiles - 1 - j)

            @pl.when(step == 1)
            def _():
                multiply(0, j)
                multiply(0, tiles - 1 - j)

            @pl.when(step > 1)
            def _():
                ring_sent(step - 2, j)

            @pl.when(jnp.logical_and(step == 1, j == 2))
            def _():
                up_copy(0, half).wait_recv()
                multiply(1, half)

            @pl.when(jnp.logical_and(step == 2, j == 0))
            def _():
                pl.semaphore_wait(relay, line - 1)
                send_plane(0)

            @pl.when(jnp.logical_and(step == 2, j == 2))
            def _():
                send_rows(0)
                plane_sent(0)

            @pl.when(jnp.logical_and(step == planes // 2 + 1, j == 0))
            def _():
                send_plane(planes // 2)

            @pl.when(jnp.logical_and(step == planes // 2 + 1, j == 2))
            def _():
                send_rows(planes // 2)
                plane_sent(planes // 2)

            @pl.when(jnp.logical_and(step > planes // 2 + 1, j == 0))
            def _():
                send_plane(step - 1)
                send_plane(planes - step + 1)

            @pl.when(jnp.logical_and(step > planes // 2 + 1, j == 2))
            def _():
                send_rows(step - 1)
                send_rows(planes - step + 1)
                plane_sent(step - 1)
                plane_sent(planes - step + 1)

        @pl.when(step == 1)
        def _():
            send_pair(0)

        @pl.when(step == planes // 2)
        def _():
            send_pair(planes // 2)

        @pl.when(step > planes // 2)
        def _():
            send_pair(step)
            send_pair(planes - step)

    down_copy(0, half - 1, a_tile(half - 1)).start()

    @pl.loop(0, half - 1)
    def _(j):
        down_copy(last - 1, tiles - 1 - j).wait_recv()
        multiply(1, tiles - 1 - j)

        @pl.when(j > 0)
        def _():
            up_copy(last - 1, j - 1).wait_recv()
            multiply(last, j - 1)

        @pl.when(j == 0)
        def _():
            send_plane(last - 1)
            send_plane(2)

        @pl.when(j == half - 2)
        def _():
            send_pair(1)

    send_rows(last - 1)
    send_rows(2)
    plane_sent(last - 1)
    plane_sent(2)
    send_plane(1)
    for slot in sorted(range(2, last), key=lambda d: abs(planes // 2 - d)):
        row_copy(slot).start()

    up_copy(last - 1, half - 2).wait_recv()
    multiply(last, half - 2)
    down_copy(0, half - 1).wait_recv()
    multiply(last, half - 1)
    send_pair(last)

    send_direct()
    send_rows(1)
    row_copy(1).start()

    @pl.loop(0, half)
    def _(j):
        ring_sent(last - 2, j)

    @pl.loop(0, half - 1)
    def _(j):
        ring_sent(last - 1, j)

    up_copy(0, half).wait_send()
    down_copy(0, half - 1).wait_send()
    plane_sent(1)
    pair_copy(last).wait_send()

    @pl.loop(1, last)
    def _(slot):
        take_rows(slot)
        row_copy(slot).wait_send()

    take_direct()
    direct_whole().wait_send()


def solution(mesh):
    planes, chips = mesh.shape["ab"], mesh.shape["cd"] // 2

    def per_device(amplitudes, integrals, live_tiles, residual_in):
        rows, depth = amplitudes.shape
        tiles, columns = depth // TILE, integrals.shape[1]
        f32, bf16 = jnp.float32, jnp.bfloat16
        dma = pltpu.SemaphoreType.DMA
        ladder = pl.pallas_call(
            functools.partial(kernel, planes, chips, math.isqrt(chips), tiles),
            out_shape=pltpu.VMEM(residual_in.shape, f32),
            in_specs=[
                pl.BlockSpec(memory_space=pltpu.HBM),
                pl.BlockSpec(memory_space=pltpu.HBM),
                pl.BlockSpec(memory_space=pltpu.HBM),
            ],
            out_specs=pl.BlockSpec(memory_space=pltpu.VMEM),
            scratch_shapes=[
                pltpu.VMEM((planes, tiles, rows, TILE), f32),
                pltpu.VMEM((tiles, TILE, columns), f32),
                pltpu.VMEM((tiles, TILE, columns), bf16),
                pltpu.VMEM((tiles, TILE, columns), bf16),
                pltpu.VMEM((planes, 2, rows, HALF), f32),
                pltpu.VMEM((planes, 2, rows, HALF), f32),
                pltpu.VMEM((planes, rows, HALF), f32),
                pltpu.VMEM((planes, (chips - 1) * 8, HALF), f32),
                pltpu.VMEM((planes, 8, HALF), f32),
                pltpu.VMEM((planes, 8, HALF), f32),
                pltpu.VMEM((chips * 8, HALF), f32),
                pltpu.SMEM((tiles,), jnp.int32),
                pltpu.SemaphoreType.REGULAR,
                dma(()),
                dma((tiles,)),
                dma((tiles,)),
                dma((planes - 1, tiles)),
                dma((planes - 1, tiles)),
                dma((planes - 1, tiles)),
                dma((planes - 1, tiles)),
                dma((planes,)),
                dma((planes,)),
                dma((planes,)),
                dma((planes,)),
                dma((planes,)),
                dma((planes,)),
                dma(()),
                dma(()),
            ],
            compiler_params=pltpu.CompilerParams(
                collective_id=0, has_side_effects=True, vmem_limit_bytes=58 * 1024 * 1024
            ),
            cost_estimate=pl.CostEstimate(
                flops=6 * planes * rows * depth * columns,
                bytes_accessed=4 * depth * (rows + columns),
                transcendentals=0,
            ),
        )(amplitudes, integrals, live_tiles)
        return residual_in + ladder

    return jax.shard_map(
        per_device,
        mesh=mesh,
        in_specs=(P("ab", "cd"), P("cd", "ab"), P("cd"), P(("ab", "cd"), None)),
        out_specs=P(("ab", "cd"), None),
        check_vma=False,
    )
```

```python
import functools
import math

import jax
import jax.numpy as jnp
from jax import lax
from jax.experimental import pallas as pl
from jax.experimental.pallas import tpu as pltpu
from jax.sharding import PartitionSpec as P

TILE = 256
HALF = 256
MESH = pl.DeviceIdType.MESH


def kernel(
    planes,
    chips,
    line,
    tiles,
    a_ref,
    b_ref,
    live_ref,
    out_ref,
    a_all,
    b_raw,
    b_hi,
    b_lo,
    part,
    folded,
    pair_recv,
    plane_recv,
    summed,
    land,
    direct,
    live,
    relay,
    live_sem,
    a_sem,
    b_sem,
    up_send,
    up_recv,
    down_send,
    down_recv,
    pair_send,
    pair_got,
    plane_send,
    plane_got,
    row_send,
    row_got,
    direct_send,
    direct_got,
):
    cd = lax.axis_index("cd")
    z = planes - 1 - lax.axis_index("ab")
    chip, core = cd // 2, cd % 2
    twin = cd + 1 - 2 * core
    above, below = (z + 1) % planes, (z + planes - 1) % planes
    half = tiles // 2
    last = planes - 1
    rows = a_ref.shape[0]

    barrier = pltpu.get_barrier_semaphore()

    def greet(cd_at, z_at):
        pl.semaphore_signal(barrier, inc=1, device_id={"cd": cd_at, "ab": planes - 1 - z_at}, device_id_type=MESH)

    greet(cd, above)
    greet(cd, below)
    greet(twin, z)

    across, along = chip // line, chip % line

    def in_row(d):
        return (across * line + (along + d) % line) * 2 + core

    def in_column(d):
        return ((across + d) % line * line + along) * 2 + core

    @pl.loop(1, line)
    def _(d):
        greet(in_row(d), z)
        greet(in_column(d), z)

    def a_tile(t):
        return a_ref.at[:, pl.ds(pl.multiple_of(t * TILE, TILE), TILE)]

    def own_copy(t):
        return pltpu.make_async_copy(a_tile(t), a_all.at[0, t], a_sem.at[t])

    def b_copy(t):
        return pltpu.make_async_copy(
            b_ref.at[pl.ds(pl.multiple_of(t * TILE, TILE), TILE), :], b_raw.at[t], b_sem.at[t]
        )

    pl.semaphore_wait(barrier, 3 + 2 * (line - 1))

    def up_copy(step, t, src=None):
        return pltpu.make_async_remote_copy(
            src_ref=a_all.at[step, t] if src is None else src,
            dst_ref=a_all.at[step + 1, t],
            send_sem=up_send.at[step, t],
            recv_sem=up_recv.at[step, t],
            device_id={"cd": cd, "ab": planes - 1 - above},
            device_id_type=MESH,
        )

    def down_copy(step, t, src=None):
        return pltpu.make_async_remote_copy(
            src_ref=a_all.at[(planes - step) % planes, t] if src is None else src,
            dst_ref=a_all.at[planes - 1 - step, t],
            send_sem=down_send.at[step, t],
            recv_sem=down_recv.at[step, t],
            device_id={"cd": cd, "ab": planes - 1 - below},
            device_id_type=MESH,
        )

    @pl.loop(0, half)
    def _(t):
        up_copy(0, t, a_tile(t)).start()
        down_copy(0, tiles - 1 - t, a_tile(tiles - 1 - t)).start()

    up_copy(0, half, a_tile(half)).start()

    @pl.loop(1, line)
    def _(d):
        pl.semaphore_signal(relay, inc=1, device_id={"cd": in_row(d), "ab": planes - 1 - z}, device_id_type=MESH)

    live_copy = pltpu.make_async_copy(live_ref, live, live_sem)
    live_copy.start()

    @pl.loop(0, tiles)
    def _(t):
        own_copy(t).start()
        b_copy(t).start()

    part[...] = jnp.zeros_like(part)

    live_copy.wait()

    @pl.loop(0, tiles)
    def _(t):
        b_copy(t).wait()
        weight = live[t].astype(jnp.float32)
        whole = b_raw[t] * weight
        high = whole.astype(jnp.bfloat16)
        b_hi[t] = high
        b_lo[t] = (whole - high.astype(jnp.float32)).astype(jnp.bfloat16)

    def multiply(slot, t):
        whole = a_all[slot, t]
        high = whole.astype(jnp.bfloat16)
        low = (whole - high.astype(jnp.float32)).astype(jnp.bfloat16)
        both = jnp.concatenate([high, low], axis=0)
        for h in range(2):
            cols = slice(h * HALF, (h + 1) * HALF)
            first = jnp.dot(both, b_hi[t, :, cols], preferred_element_type=jnp.float32)
            second = jnp.dot(high, b_lo[t, :, cols], preferred_element_type=jnp.float32)
            part[slot, h] += first[:rows] + (first[rows:] + second)

    def pair_copy(slot):
        return pltpu.make_async_remote_copy(
            src_ref=folded.at[slot, 1 - core],
            dst_ref=pair_recv.at[slot],
            send_sem=pair_send.at[slot],
            recv_sem=pair_got.at[slot],
            device_id={"cd": twin, "ab": planes - 1 - z},
            device_id_type=MESH,
        )

    def plane_copy(slot, d):
        to = (chip + d) % chips
        return pltpu.make_async_remote_copy(
            src_ref=folded.at[slot, core, pl.ds(pl.multiple_of(to * 8, 8), 8)],
            dst_ref=plane_recv.at[slot, pl.ds(pl.multiple_of((d - 1) * 8, 8), 8)],
            send_sem=plane_send.at[slot],
            recv_sem=plane_got.at[slot],
            device_id={"cd": to * 2 + core, "ab": planes - 1 - z},
            device_id_type=MESH,
        )

    def plane_whole(slot):
        return pltpu.make_async_remote_copy(
            src_ref=folded.at[slot, core, pl.ds(0, (chips - 1) * 8)],
            dst_ref=plane_recv.at[slot],
            send_sem=plane_send.at[slot],
            recv_sem=plane_got.at[slot],
            device_id={"cd": twin, "ab": planes - 1 - z},
            device_id_type=MESH,
        )

    def row_copy(slot):
        return pltpu.make_async_remote_copy(
            src_ref=summed.at[slot],
            dst_ref=land.at[slot],
            send_sem=row_send.at[slot],
            recv_sem=row_got.at[slot],
            device_id={"cd": cd, "ab": planes - 1 - (z + planes - slot) % planes},
            device_id_type=MESH,
        )

    away = sorted(
        ((dx, dy) for dx in range(line) for dy in range(line)),
        key=lambda d: -min(d[0], line - d[0]) - min(d[1], line - d[1]),
    )

    def direct_copy(at):
        dx, dy = away[at]
        to = (across + dx) % line * line + (along + dy) % line
        return pltpu.make_async_remote_copy(
            src_ref=folded.at[last, core, pl.ds(pl.multiple_of(to * 8, 8), 8)],
            dst_ref=direct.at[pl.ds(at * 8, 8)],
            send_sem=direct_send,
            recv_sem=direct_got,
            device_id={"cd": to * 2 + core, "ab": planes - 1 - above},
            device_id_type=MESH,
        )

    def direct_whole():
        return pltpu.make_async_remote_copy(
            src_ref=folded.at[last, core],
            dst_ref=direct,
            send_sem=direct_send,
            recv_sem=direct_got,
            device_id={"cd": cd, "ab": planes - 1 - above},
            device_id_type=MESH,
        )

    def send_direct():
        pair_copy(last).wait_recv()
        folded[last, core] += pair_recv[last]
        for at in range(chips):
            direct_copy(at).start()

    def take_direct():
        direct_whole().wait_recv()
        write_rows(last, jnp.sum(direct[...].reshape(chips, 8, HALF), axis=0))

    def send_pair(slot):
        left, right = part[slot, 0], part[slot, 1]
        upper = lax.broadcasted_iota(jnp.int32, left.shape, 0) % 8 < 4
        folded[slot, 0] = jnp.where(upper, left, pltpu.roll(right, 4, 0))
        folded[slot, 1] = jnp.where(upper, pltpu.roll(left, rows - 4, 0), right)
        pair_copy(slot).start()

    def send_plane(slot):
        pair_copy(slot).wait_recv()
        folded[slot, core] += pair_recv[slot]

        @pl.loop(1, chips)
        def _(d):
            plane_copy(slot, d).start()

    def write_rows(slot, got):
        first = (planes - 1 - (z + slot) % planes) * (2 * HALF)
        for h in range(2):
            cols = pl.ds(pl.multiple_of(first + h * HALF, HALF), HALF)
            out_ref[:, cols] = got[4 * h : 4 * h + 4]

    def send_rows(slot):
        plane_whole(slot).wait_recv()
        mine = folded[slot, core, pl.ds(pl.multiple_of(chip * 8, 8), 8)]
        total = mine + jnp.sum(plane_recv[slot].reshape(chips - 1, 8, HALF), axis=0)
        if isinstance(slot, int) and slot == 0:
            write_rows(0, total)
        else:
            summed[slot] = total

    def take_rows(slot):
        row_copy(slot).wait_recv()
        write_rows(slot, land[slot])

    @pl.loop(0, tiles)
    def _(t):
        own_copy(t).wait()

    def forward_up(step, j):
        up_copy(step - 1, j).wait_recv()

        @pl.when(jnp.logical_or(step < last - 1, jnp.logical_and(step < last, j < half - 1)))
        def _():
            up_copy(step, j).start()

    def forward_down(step, j):
        down_copy(step - 1, tiles - 1 - j).wait_recv()

        @pl.when(jnp.logical_or(step < last - 1, jnp.logical_and(step < last, j < half - 1)))
        def _():
            down_copy(step, tiles - 1 - j).start()

    def ring_sent(step, j):
        up_copy(step, j).wait_send()
        down_copy(step, tiles - 1 - j).wait_send()

    def plane_sent(slot):
        pair_copy(slot).wait_send()
        plane_whole(slot).wait_send()

    @pl.loop(1, last)
    def _(step):
        @pl.loop(0, half)
        def _(j):
            forward_up(step, j)
            forward_down(step, j)
            multiply(step, j)
            multiply(planes - step, tiles - 1 - j)

            @pl.when(step == 1)
            def _():
                multiply(0, j)
                multiply(0, tiles - 1 - j)

            @pl.when(step > 1)
            def _():
                ring_sent(step - 2, j)

            @pl.when(jnp.logical_and(step == 1, j == 2))
            def _():
                up_copy(0, half).wait_recv()
                multiply(1, half)

            @pl.when(jnp.logical_and(step == 2, j == 0))
            def _():
                pl.semaphore_wait(relay, line - 1)
                send_plane(0)

            @pl.when(jnp.logical_and(step == 2, j == 2))
            def _():
                send_rows(0)
                plane_sent(0)

            @pl.when(jnp.logical_and(step == planes // 2 + 1, j == 0))
            def _():
                send_plane(planes // 2)

            @pl.when(jnp.logical_and(step == planes // 2 + 1, j == 2))
            def _():
                send_rows(planes // 2)
                plane_sent(planes // 2)

            @pl.when(jnp.logical_and(step > planes // 2 + 1, j == 0))
            def _():
                send_plane(step - 1)
                send_plane(planes - step + 1)

            @pl.when(jnp.logical_and(step > planes // 2 + 1, j == 2))
            def _():
                send_rows(step - 1)
                send_rows(planes - step + 1)
                plane_sent(step - 1)
                plane_sent(planes - step + 1)

        @pl.when(step == 1)
        def _():
            send_pair(0)

        @pl.when(step == planes // 2)
        def _():
            send_pair(planes // 2)

        @pl.when(step > planes // 2)
        def _():
            send_pair(step)
            send_pair(planes - step)

    down_copy(0, half - 1, a_tile(half - 1)).start()

    @pl.loop(0, half - 1)
    def _(j):
        down_copy(last - 1, tiles - 1 - j).wait_recv()
        multiply(1, tiles - 1 - j)

        @pl.when(j > 0)
        def _():
            up_copy(last - 1, j - 1).wait_recv()
            multiply(last, j - 1)

        @pl.when(j == 0)
        def _():
            send_plane(last - 1)
            send_plane(2)

        @pl.when(j == half - 2)
        def _():
            send_pair(1)

    send_rows(last - 1)
    send_rows(2)
    plane_sent(last - 1)
    plane_sent(2)
    send_plane(1)
    for slot in sorted(range(2, last), key=lambda d: abs(planes // 2 - d)):
        row_copy(slot).start()

    up_copy(last - 1, half - 2).wait_recv()
    multiply(last, half - 2)
    down_copy(0, half - 1).wait_recv()
    multiply(last, half - 1)
    send_pair(last)

    send_direct()
    send_rows(1)
    row_copy(1).start()

    @pl.loop(0, half)
    def _(j):
        ring_sent(last - 2, j)

    @pl.loop(0, half - 1)
    def _(j):
        ring_sent(last - 1, j)

    up_copy(0, half).wait_send()
    down_copy(0, half - 1).wait_send()
    plane_sent(1)
    pair_copy(last).wait_send()

    @pl.loop(1, last)
    def _(slot):
        take_rows(slot)
        row_copy(slot).wait_send()

    take_direct()
    direct_whole().wait_send()


def solution(mesh):
    planes, chips = mesh.shape["ab"], mesh.shape["cd"] // 2

    def per_device(amplitudes, integrals, live_tiles, residual_in):
        rows, depth = amplitudes.shape
        tiles, columns = depth // TILE, integrals.shape[1]
        f32, bf16 = jnp.float32, jnp.bfloat16
        dma = pltpu.SemaphoreType.DMA
        ladder = pl.pallas_call(
            functools.partial(kernel, planes, chips, math.isqrt(chips), tiles),
            out_shape=pltpu.VMEM(residual_in.shape, f32),
            in_specs=[
                pl.BlockSpec(memory_space=pltpu.HBM),
                pl.BlockSpec(memory_space=pltpu.HBM),
                pl.BlockSpec(memory_space=pltpu.HBM),
            ],
            out_specs=pl.BlockSpec(memory_space=pltpu.VMEM),
            scratch_shapes=[
                pltpu.VMEM((planes, tiles, rows, TILE), f32),
                pltpu.VMEM((tiles, TILE, columns), f32),
                pltpu.VMEM((tiles, TILE, columns), bf16),
                pltpu.VMEM((tiles, TILE, columns), bf16),
                pltpu.VMEM((planes, 2, rows, HALF), f32),
                pltpu.VMEM((planes, 2, rows, HALF), f32),
                pltpu.VMEM((planes, rows, HALF), f32),
                pltpu.VMEM((planes, (chips - 1) * 8, HALF), f32),
                pltpu.VMEM((planes, 8, HALF), f32),
                pltpu.VMEM((planes, 8, HALF), f32),
                pltpu.VMEM((chips * 8, HALF), f32),
                pltpu.SMEM((tiles,), jnp.int32),
                pltpu.SemaphoreType.REGULAR,
                dma(()),
                dma((tiles,)),
                dma((tiles,)),
                dma((planes - 1, tiles)),
                dma((planes - 1, tiles)),
                dma((planes - 1, tiles)),
                dma((planes - 1, tiles)),
                dma((planes,)),
                dma((planes,)),
                dma((planes,)),
                dma((planes,)),
                dma((planes,)),
                dma((planes,)),
                dma(()),
                dma(()),
            ],
            compiler_params=pltpu.CompilerParams(
                collective_id=0, has_side_effects=True, vmem_limit_bytes=58 * 1024 * 1024
            ),
            cost_estimate=pl.CostEstimate(
                flops=6 * planes * rows * depth * columns,
                bytes_accessed=4 * depth * (rows + columns),
                transcendentals=0,
            ),
        )(amplitudes, integrals, live_tiles)
        return residual_in + ladder

    return jax.shard_map(
        per_device,
        mesh=mesh,
        in_specs=(P("ab", "cd"), P("cd", "ab"), P("cd"), P(("ab", "cd"), None)),
        out_specs=P(("ab", "cd"), None),
        check_vma=False,
    )
```

```python
import functools
import math

import jax
import jax.numpy as jnp
from jax import lax
from jax.experimental import pallas as pl
from jax.experimental.pallas import tpu as pltpu
from jax.sharding import PartitionSpec as P

TILE = 256
HALF = 256
MESH = pl.DeviceIdType.MESH


def kernel(
    planes,
    chips,
    line,
    tiles,
    a_ref,
    b_ref,
    live_ref,
    out_ref,
    a_all,
    b_raw,
    b_hi,
    b_lo,
    part,
    folded,
    pair_recv,
    plane_recv,
    summed,
    land,
    direct,
    live,
    relay,
    live_sem,
    a_sem,
    b_sem,
    up_send,
    up_recv,
    down_send,
    down_recv,
    pair_send,
    pair_got,
    plane_send,
    plane_got,
    row_send,
    row_got,
    direct_send,
    direct_got,
):
    cd = lax.axis_index("cd")
    z = planes - 1 - lax.axis_index("ab")
    chip, core = cd // 2, cd % 2
    twin = cd + 1 - 2 * core
    above, below = (z + 1) % planes, (z + planes - 1) % planes
    half = tiles // 2
    last = planes - 1
    rows = a_ref.shape[0]

    barrier = pltpu.get_barrier_semaphore()

    def greet(cd_at, z_at):
        pl.semaphore_signal(barrier, inc=1, device_id={"cd": cd_at, "ab": planes - 1 - z_at}, device_id_type=MESH)

    greet(cd, above)
    greet(cd, below)
    greet(twin, z)

    across, along = chip // line, chip % line

    def in_row(d):
        return (across * line + (along + d) % line) * 2 + core

    def in_column(d):
        return ((across + d) % line * line + along) * 2 + core

    @pl.loop(1, line)
    def _(d):
        greet(in_row(d), z)
        greet(in_column(d), z)

    def a_tile(t):
        return a_ref.at[:, pl.ds(pl.multiple_of(t * TILE, TILE), TILE)]

    def own_copy(t):
        return pltpu.make_async_copy(a_tile(t), a_all.at[0, t], a_sem.at[t])

    def b_copy(t):
        return pltpu.make_async_copy(
            b_ref.at[pl.ds(pl.multiple_of(t * TILE, TILE), TILE), :], b_raw.at[t], b_sem.at[t]
        )

    pl.semaphore_wait(barrier, 3 + 2 * (line - 1))

    def up_copy(step, t, src=None):
        return pltpu.make_async_remote_copy(
            src_ref=a_all.at[step, t] if src is None else src,
            dst_ref=a_all.at[step + 1, t],
            send_sem=up_send.at[step, t],
            recv_sem=up_recv.at[step, t],
            device_id={"cd": cd, "ab": planes - 1 - above},
            device_id_type=MESH,
        )

    def down_copy(step, t, src=None):
        return pltpu.make_async_remote_copy(
            src_ref=a_all.at[(planes - step) % planes, t] if src is None else src,
            dst_ref=a_all.at[planes - 1 - step, t],
            send_sem=down_send.at[step, t],
            recv_sem=down_recv.at[step, t],
            device_id={"cd": cd, "ab": planes - 1 - below},
            device_id_type=MESH,
        )

    @pl.loop(0, half)
    def _(t):
        up_copy(0, t, a_tile(t)).start()
        down_copy(0, tiles - 1 - t, a_tile(tiles - 1 - t)).start()

    up_copy(0, half, a_tile(half)).start()

    @pl.loop(1, line)
    def _(d):
        pl.semaphore_signal(relay, inc=1, device_id={"cd": in_row(d), "ab": planes - 1 - z}, device_id_type=MESH)

    live_copy = pltpu.make_async_copy(live_ref, live, live_sem)
    live_copy.start()

    @pl.loop(0, tiles)
    def _(t):
        own_copy(t).start()
        b_copy(t).start()

    part[...] = jnp.zeros_like(part)

    live_copy.wait()

    @pl.loop(0, tiles)
    def _(t):
        b_copy(t).wait()
        weight = live[t].astype(jnp.float32)
        whole = b_raw[t] * weight
        high = whole.astype(jnp.bfloat16)
        b_hi[t] = high
        b_lo[t] = (whole - high.astype(jnp.float32)).astype(jnp.bfloat16)

    def multiply(slot, t):
        whole = a_all[slot, t]
        high = whole.astype(jnp.bfloat16)
        low = (whole - high.astype(jnp.float32)).astype(jnp.bfloat16)
        both = jnp.concatenate([high, low], axis=0)
        for h in range(2):
            cols = slice(h * HALF, (h + 1) * HALF)
            first = jnp.dot(both, b_hi[t, :, cols], preferred_element_type=jnp.float32)
            second = jnp.dot(high, b_lo[t, :, cols], preferred_element_type=jnp.float32)
            part[slot, h] += first[:rows] + (first[rows:] + second)

    def pair_copy(slot):
        return pltpu.make_async_remote_copy(
            src_ref=folded.at[slot, 1 - core],
            dst_ref=pair_recv.at[slot],
            send_sem=pair_send.at[slot],
            recv_sem=pair_got.at[slot],
            device_id={"cd": twin, "ab": planes - 1 - z},
            device_id_type=MESH,
        )

    def plane_copy(slot, d):
        to = (chip + d) % chips
        return pltpu.make_async_remote_copy(
            src_ref=folded.at[slot, core, pl.ds(pl.multiple_of(to * 8, 8), 8)],
            dst_ref=plane_recv.at[slot, pl.ds(pl.multiple_of((d - 1) * 8, 8), 8)],
            send_sem=plane_send.at[slot],
            recv_sem=plane_got.at[slot],
            device_id={"cd": to * 2 + core, "ab": planes - 1 - z},
            device_id_type=MESH,
        )

    def plane_whole(slot):
        return pltpu.make_async_remote_copy(
            src_ref=folded.at[slot, core, pl.ds(0, (chips - 1) * 8)],
            dst_ref=plane_recv.at[slot],
            send_sem=plane_send.at[slot],
            recv_sem=plane_got.at[slot],
            device_id={"cd": twin, "ab": planes - 1 - z},
            device_id_type=MESH,
        )

    def row_copy(slot):
        return pltpu.make_async_remote_copy(
            src_ref=summed.at[slot],
            dst_ref=land.at[slot],
            send_sem=row_send.at[slot],
            recv_sem=row_got.at[slot],
            device_id={"cd": cd, "ab": planes - 1 - (z + planes - slot) % planes},
            device_id_type=MESH,
        )

    away = sorted(
        ((dx, dy) for dx in range(line) for dy in range(line)),
        key=lambda d: -min(d[0], line - d[0]) - min(d[1], line - d[1]),
    )

    def direct_copy(way, at):
        dx, dy = away[at]
        to = (across + dx) % line * line + (along + dy) % line
        return pltpu.make_async_remote_copy(
            src_ref=folded.at[(last, 1)[way], core, pl.ds(pl.multiple_of(to * 8, 8), 8)],
            dst_ref=direct.at[way, pl.ds(at * 8, 8)],
            send_sem=direct_send.at[way],
            recv_sem=direct_got.at[way],
            device_id={"cd": to * 2 + core, "ab": planes - 1 - (above, below)[way]},
            device_id_type=MESH,
        )

    def direct_whole(way):
        return pltpu.make_async_remote_copy(
            src_ref=folded.at[(last, 1)[way], core],
            dst_ref=direct.at[way],
            send_sem=direct_send.at[way],
            recv_sem=direct_got.at[way],
            device_id={"cd": cd, "ab": planes - 1 - (above, below)[way]},
            device_id_type=MESH,
        )

    def send_direct(way):
        slot = (last, 1)[way]
        pair_copy(slot).wait_recv()
        folded[slot, core] += pair_recv[slot]
        for at in range(chips):
            direct_copy(way, at).start()

    def take_direct(way):
        direct_whole(way).wait_recv()
        write_rows((last, 1)[way], jnp.sum(direct[way].reshape(chips, 8, HALF), axis=0))

    def send_pair(slot):
        left, right = part[slot, 0], part[slot, 1]
        upper = lax.broadcasted_iota(jnp.int32, left.shape, 0) % 8 < 4
        folded[slot, 0] = jnp.where(upper, left, pltpu.roll(right, 4, 0))
        folded[slot, 1] = jnp.where(upper, pltpu.roll(left, rows - 4, 0), right)
        pair_copy(slot).start()

    def send_plane(slot):
        pair_copy(slot).wait_recv()
        folded[slot, core] += pair_recv[slot]

        @pl.loop(1, chips)
        def _(d):
            plane_copy(slot, d).start()

    def write_rows(slot, got):
        first = (planes - 1 - (z + slot) % planes) * (2 * HALF)
        for h in range(2):
            cols = pl.ds(pl.multiple_of(first + h * HALF, HALF), HALF)
            out_ref[:, cols] = got[4 * h : 4 * h + 4]

    def send_rows(slot):
        plane_whole(slot).wait_recv()
        mine = folded[slot, core, pl.ds(pl.multiple_of(chip * 8, 8), 8)]
        total = mine + jnp.sum(plane_recv[slot].reshape(chips - 1, 8, HALF), axis=0)
        if isinstance(slot, int) and slot == 0:
            write_rows(0, total)
        else:
            summed[slot] = total

    def take_rows(slot):
        row_copy(slot).wait_recv()
        write_rows(slot, land[slot])

    @pl.loop(0, tiles)
    def _(t):
        own_copy(t).wait()

    def forward_up(step, j):
        up_copy(step - 1, j).wait_recv()

        @pl.when(jnp.logical_or(step < last - 1, jnp.logical_and(step < last, j < half - 1)))
        def _():
            up_copy(step, j).start()

    def forward_down(step, j):
        down_copy(step - 1, tiles - 1 - j).wait_recv()

        @pl.when(jnp.logical_or(step < last - 1, jnp.logical_and(step < last, j < half - 1)))
        def _():
            down_copy(step, tiles - 1 - j).start()

    def ring_sent(step, j):
        up_copy(step, j).wait_send()
        down_copy(step, tiles - 1 - j).wait_send()

    def plane_sent(slot):
        pair_copy(slot).wait_send()
        plane_whole(slot).wait_send()

    @pl.loop(1, last)
    def _(step):
        @pl.loop(0, half)
        def _(j):
            forward_up(step, j)
            forward_down(step, j)
            multiply(step, j)
            multiply(planes - step, tiles - 1 - j)

            @pl.when(step == 1)
            def _():
                multiply(0, j)
                multiply(0, tiles - 1 - j)

            @pl.when(step > 1)
            def _():
                ring_sent(step - 2, j)

            @pl.when(jnp.logical_and(step == 1, j == 2))
            def _():
                up_copy(0, half).wait_recv()
                multiply(1, half)

            @pl.when(jnp.logical_and(step == 2, j == 0))
            def _():
                pl.semaphore_wait(relay, line - 1)
                send_plane(0)

            @pl.when(jnp.logical_and(step == 2, j == 2))
            def _():
                send_rows(0)
                plane_sent(0)

            @pl.when(jnp.logical_and(step == planes // 2 + 1, j == 0))
            def _():
                send_plane(planes // 2)

            @pl.when(jnp.logical_and(step == planes // 2 + 1, j == 2))
            def _():
                send_rows(planes // 2)
                plane_sent(planes // 2)

            @pl.when(jnp.logical_and(step > planes // 2 + 1, j == 0))
            def _():
                send_plane(step - 1)
                send_plane(planes - step + 1)

            @pl.when(jnp.logical_and(step > planes // 2 + 1, j == 2))
            def _():
                send_rows(step - 1)
                send_rows(planes - step + 1)
                plane_sent(step - 1)
                plane_sent(planes - step + 1)

        @pl.when(step == 1)
        def _():
            send_pair(0)

        @pl.when(step == planes // 2)
        def _():
            send_pair(planes // 2)

        @pl.when(step > planes // 2)
        def _():
            send_pair(step)
            send_pair(planes - step)

    down_copy(0, half - 1, a_tile(half - 1)).start()

    @pl.loop(0, half - 1)
    def _(j):
        down_copy(last - 1, tiles - 1 - j).wait_recv()
        multiply(1, tiles - 1 - j)

        @pl.when(j > 0)
        def _():
            up_copy(last - 1, j - 1).wait_recv()
            multiply(last, j - 1)

        @pl.when(j == 0)
        def _():
            send_plane(last - 1)
            send_plane(2)

        @pl.when(j == half - 2)
        def _():
            send_pair(1)

    send_rows(last - 1)
    send_rows(2)
    send_direct(1)
    plane_sent(last - 1)
    plane_sent(2)
    for slot in sorted(range(2, last), key=lambda d: abs(planes // 2 - d)):
        row_copy(slot).start()

    up_copy(last - 1, half - 2).wait_recv()
    multiply(last, half - 2)
    down_copy(0, half - 1).wait_recv()
    multiply(last, half - 1)
    send_pair(last)

    send_direct(0)

    @pl.loop(0, half)
    def _(j):
        ring_sent(last - 2, j)

    @pl.loop(0, half - 1)
    def _(j):
        ring_sent(last - 1, j)

    up_copy(0, half).wait_send()
    down_copy(0, half - 1).wait_send()
    pair_copy(1).wait_send()
    pair_copy(last).wait_send()

    take_direct(1)

    @pl.loop(2, last)
    def _(slot):
        take_rows(slot)
        row_copy(slot).wait_send()

    take_direct(0)
    direct_whole(1).wait_send()
    direct_whole(0).wait_send()


def solution(mesh):
    planes, chips = mesh.shape["ab"], mesh.shape["cd"] // 2

    def per_device(amplitudes, integrals, live_tiles, residual_in):
        rows, depth = amplitudes.shape
        tiles, columns = depth // TILE, integrals.shape[1]
        f32, bf16 = jnp.float32, jnp.bfloat16
        dma = pltpu.SemaphoreType.DMA
        ladder = pl.pallas_call(
            functools.partial(kernel, planes, chips, math.isqrt(chips), tiles),
            out_shape=pltpu.VMEM(residual_in.shape, f32),
            in_specs=[
                pl.BlockSpec(memory_space=pltpu.HBM),
                pl.BlockSpec(memory_space=pltpu.HBM),
                pl.BlockSpec(memory_space=pltpu.HBM),
            ],
            out_specs=pl.BlockSpec(memory_space=pltpu.VMEM),
            scratch_shapes=[
                pltpu.VMEM((planes, tiles, rows, TILE), f32),
                pltpu.VMEM((tiles, TILE, columns), f32),
                pltpu.VMEM((tiles, TILE, columns), bf16),
                pltpu.VMEM((tiles, TILE, columns), bf16),
                pltpu.VMEM((planes, 2, rows, HALF), f32),
                pltpu.VMEM((planes, 2, rows, HALF), f32),
                pltpu.VMEM((planes, rows, HALF), f32),
                pltpu.VMEM((planes, (chips - 1) * 8, HALF), f32),
                pltpu.VMEM((planes, 8, HALF), f32),
                pltpu.VMEM((planes, 8, HALF), f32),
                pltpu.VMEM((2, chips * 8, HALF), f32),
                pltpu.SMEM((tiles,), jnp.int32),
                pltpu.SemaphoreType.REGULAR,
                dma(()),
                dma((tiles,)),
                dma((tiles,)),
                dma((planes - 1, tiles)),
                dma((planes - 1, tiles)),
                dma((planes - 1, tiles)),
                dma((planes - 1, tiles)),
                dma((planes,)),
                dma((planes,)),
                dma((planes,)),
                dma((planes,)),
                dma((planes,)),
                dma((planes,)),
                dma((2,)),
                dma((2,)),
            ],
            compiler_params=pltpu.CompilerParams(
                collective_id=0, has_side_effects=True, vmem_limit_bytes=58 * 1024 * 1024
            ),
            cost_estimate=pl.CostEstimate(
                flops=6 * planes * rows * depth * columns,
                bytes_accessed=4 * depth * (rows + columns),
                transcendentals=0,
            ),
        )(amplitudes, integrals, live_tiles)
        return residual_in + ladder

    return jax.shard_map(
        per_device,
        mesh=mesh,
        in_specs=(P("ab", "cd"), P("cd", "ab"), P("cd"), P(("ab", "cd"), None)),
        out_specs=P(("ab", "cd"), None),
        check_vma=False,
    )
```

```python
import functools
import math

import jax
import jax.numpy as jnp
from jax import lax
from jax.experimental import pallas as pl
from jax.experimental.pallas import tpu as pltpu
from jax.sharding import PartitionSpec as P

TILE = 256
HALF = 256
MESH = pl.DeviceIdType.MESH


def kernel(
    planes,
    chips,
    line,
    tiles,
    a_ref,
    b_ref,
    live_ref,
    out_ref,
    a_all,
    b_raw,
    b_hi,
    b_lo,
    part,
    folded,
    pair_recv,
    plane_recv,
    summed,
    land,
    direct,
    live,
    relay,
    live_sem,
    a_sem,
    b_sem,
    up_send,
    up_recv,
    down_send,
    down_recv,
    pair_send,
    pair_got,
    plane_send,
    plane_got,
    row_send,
    row_got,
    direct_send,
    direct_got,
):
    cd = lax.axis_index("cd")
    z = planes - 1 - lax.axis_index("ab")
    chip, core = cd // 2, cd % 2
    twin = cd + 1 - 2 * core
    above, below = (z + 1) % planes, (z + planes - 1) % planes
    half = tiles // 2
    last = planes - 1
    rows = a_ref.shape[0]

    barrier = pltpu.get_barrier_semaphore()

    def greet(cd_at, z_at):
        pl.semaphore_signal(barrier, inc=1, device_id={"cd": cd_at, "ab": planes - 1 - z_at}, device_id_type=MESH)

    greet(cd, above)
    greet(cd, below)
    greet(twin, z)

    across, along = chip // line, chip % line

    def in_row(d):
        return (across * line + (along + d) % line) * 2 + core

    def in_column(d):
        return ((across + d) % line * line + along) * 2 + core

    @pl.loop(1, line)
    def _(d):
        greet(in_row(d), z)
        greet(in_column(d), z)

    def a_tile(t):
        return a_ref.at[:, pl.ds(pl.multiple_of(t * TILE, TILE), TILE)]

    def own_copy(t):
        return pltpu.make_async_copy(a_tile(t), a_all.at[0, t], a_sem.at[t])

    def b_copy(t):
        return pltpu.make_async_copy(
            b_ref.at[pl.ds(pl.multiple_of(t * TILE, TILE), TILE), :], b_raw.at[t], b_sem.at[t]
        )

    pl.semaphore_wait(barrier, 3 + 2 * (line - 1))

    def up_copy(step, t, src=None):
        return pltpu.make_async_remote_copy(
            src_ref=a_all.at[step, t] if src is None else src,
            dst_ref=a_all.at[step + 1, t],
            send_sem=up_send.at[step, t],
            recv_sem=up_recv.at[step, t],
            device_id={"cd": cd, "ab": planes - 1 - above},
            device_id_type=MESH,
        )

    def down_copy(step, t, src=None):
        return pltpu.make_async_remote_copy(
            src_ref=a_all.at[(planes - step) % planes, t] if src is None else src,
            dst_ref=a_all.at[planes - 1 - step, t],
            send_sem=down_send.at[step, t],
            recv_sem=down_recv.at[step, t],
            device_id={"cd": cd, "ab": planes - 1 - below},
            device_id_type=MESH,
        )

    @pl.loop(0, half)
    def _(t):
        up_copy(0, t, a_tile(t)).start()
        down_copy(0, tiles - 1 - t, a_tile(tiles - 1 - t)).start()

    up_copy(0, half, a_tile(half)).start()

    @pl.loop(1, line)
    def _(d):
        pl.semaphore_signal(relay, inc=1, device_id={"cd": in_row(d), "ab": planes - 1 - z}, device_id_type=MESH)

    live_copy = pltpu.make_async_copy(live_ref, live, live_sem)
    live_copy.start()

    @pl.loop(0, tiles)
    def _(t):
        own_copy(t).start()
        b_copy(t).start()

    part[...] = jnp.zeros_like(part)

    live_copy.wait()

    @pl.loop(0, tiles)
    def _(t):
        b_copy(t).wait()
        weight = live[t].astype(jnp.float32)
        whole = b_raw[t] * weight
        high = whole.astype(jnp.bfloat16)
        b_hi[t] = high
        b_lo[t] = (whole - high.astype(jnp.float32)).astype(jnp.bfloat16)

    def multiply(slot, t):
        whole = a_all[slot, t]
        high = whole.astype(jnp.bfloat16)
        low = (whole - high.astype(jnp.float32)).astype(jnp.bfloat16)
        both = jnp.concatenate([high, low], axis=0)
        for h in range(2):
            cols = slice(h * HALF, (h + 1) * HALF)
            first = jnp.dot(both, b_hi[t, :, cols], preferred_element_type=jnp.float32)
            second = jnp.dot(high, b_lo[t, :, cols], preferred_element_type=jnp.float32)
            part[slot, h] += first[:rows] + (first[rows:] + second)

    def pair_copy(slot):
        return pltpu.make_async_remote_copy(
            src_ref=folded.at[slot, 1 - core],
            dst_ref=pair_recv.at[slot],
            send_sem=pair_send.at[slot],
            recv_sem=pair_got.at[slot],
            device_id={"cd": twin, "ab": planes - 1 - z},
            device_id_type=MESH,
        )

    def plane_copy(slot, d):
        to = (chip + d) % chips
        return pltpu.make_async_remote_copy(
            src_ref=folded.at[slot, core, pl.ds(pl.multiple_of(to * 8, 8), 8)],
            dst_ref=plane_recv.at[slot, pl.ds(pl.multiple_of((d - 1) * 8, 8), 8)],
            send_sem=plane_send.at[slot],
            recv_sem=plane_got.at[slot],
            device_id={"cd": to * 2 + core, "ab": planes - 1 - z},
            device_id_type=MESH,
        )

    def plane_whole(slot):
        return pltpu.make_async_remote_copy(
            src_ref=folded.at[slot, core, pl.ds(0, (chips - 1) * 8)],
            dst_ref=plane_recv.at[slot],
            send_sem=plane_send.at[slot],
            recv_sem=plane_got.at[slot],
            device_id={"cd": twin, "ab": planes - 1 - z},
            device_id_type=MESH,
        )

    def row_copy(slot):
        return pltpu.make_async_remote_copy(
            src_ref=summed.at[slot],
            dst_ref=land.at[slot],
            send_sem=row_send.at[slot],
            recv_sem=row_got.at[slot],
            device_id={"cd": cd, "ab": planes - 1 - (z + planes - slot) % planes},
            device_id_type=MESH,
        )

    away = sorted(
        ((dx, dy) for dx in range(line) for dy in range(line)),
        key=lambda d: -min(d[0], line - d[0]) - min(d[1], line - d[1]),
    )

    def direct_copy(way, at):
        dx, dy = away[at]
        to = (across + dx) % line * line + (along + dy) % line
        return pltpu.make_async_remote_copy(
            src_ref=folded.at[(last, 1)[way], core, pl.ds(pl.multiple_of(to * 8, 8), 8)],
            dst_ref=direct.at[way, pl.ds(at * 8, 8)],
            send_sem=direct_send.at[way],
            recv_sem=direct_got.at[way],
            device_id={"cd": to * 2 + core, "ab": planes - 1 - (above, below)[way]},
            device_id_type=MESH,
        )

    def direct_whole(way):
        return pltpu.make_async_remote_copy(
            src_ref=folded.at[(last, 1)[way], core],
            dst_ref=direct.at[way],
            send_sem=direct_send.at[way],
            recv_sem=direct_got.at[way],
            device_id={"cd": cd, "ab": planes - 1 - (above, below)[way]},
            device_id_type=MESH,
        )

    def send_direct(way):
        slot = (last, 1)[way]
        pair_copy(slot).wait_recv()
        folded[slot, core] += pair_recv[slot]
        for at in range(chips):
            direct_copy(way, at).start()

    def take_direct(way):
        direct_whole(way).wait_recv()
        write_rows((last, 1)[way], jnp.sum(direct[way].reshape(chips, 8, HALF), axis=0))

    def send_pair(slot):
        left, right = part[slot, 0], part[slot, 1]
        upper = lax.broadcasted_iota(jnp.int32, left.shape, 0) % 8 < 4
        folded[slot, 0] = jnp.where(upper, left, pltpu.roll(right, 4, 0))
        folded[slot, 1] = jnp.where(upper, pltpu.roll(left, rows - 4, 0), right)
        pair_copy(slot).start()

    def send_plane(slot):
        pair_copy(slot).wait_recv()
        folded[slot, core] += pair_recv[slot]

        @pl.loop(1, chips)
        def _(d):
            plane_copy(slot, d).start()

    def write_rows(slot, got):
        first = (planes - 1 - (z + slot) % planes) * (2 * HALF)
        for h in range(2):
            cols = pl.ds(pl.multiple_of(first + h * HALF, HALF), HALF)
            out_ref[:, cols] = got[4 * h : 4 * h + 4]

    def send_rows(slot):
        plane_whole(slot).wait_recv()
        mine = folded[slot, core, pl.ds(pl.multiple_of(chip * 8, 8), 8)]
        total = mine + jnp.sum(plane_recv[slot].reshape(chips - 1, 8, HALF), axis=0)
        if isinstance(slot, int) and slot == 0:
            write_rows(0, total)
        else:
            summed[slot] = total

    def take_rows(slot):
        row_copy(slot).wait_recv()
        write_rows(slot, land[slot])

    @pl.loop(0, tiles)
    def _(t):
        own_copy(t).wait()

    def forward_up(step, j):
        up_copy(step - 1, j).wait_recv()

        @pl.when(jnp.logical_or(step < last - 1, jnp.logical_and(step < last, j < half - 1)))
        def _():
            up_copy(step, j).start()

    def forward_down(step, j):
        down_copy(step - 1, tiles - 1 - j).wait_recv()

        @pl.when(jnp.logical_or(step < last - 1, jnp.logical_and(step < last, j < half - 1)))
        def _():
            down_copy(step, tiles - 1 - j).start()

    def ring_sent(step, j):
        up_copy(step, j).wait_send()
        down_copy(step, tiles - 1 - j).wait_send()

    def plane_sent(slot):
        pair_copy(slot).wait_send()
        plane_whole(slot).wait_send()

    @pl.loop(1, last)
    def _(step):
        @pl.loop(0, half)
        def _(j):
            forward_up(step, j)
            forward_down(step, j)
            multiply(step, j)
            multiply(planes - step, tiles - 1 - j)

            @pl.when(step == 1)
            def _():
                multiply(0, j)
                multiply(0, tiles - 1 - j)

            @pl.when(step > 1)
            def _():
                ring_sent(step - 2, j)

            @pl.when(jnp.logical_and(step == 1, j == 2))
            def _():
                up_copy(0, half).wait_recv()
                multiply(1, half)

            @pl.when(jnp.logical_and(step == 2, j == 0))
            def _():
                pl.semaphore_wait(relay, line - 1)
                send_plane(0)

            @pl.when(jnp.logical_and(step == 2, j == 2))
            def _():
                send_rows(0)
                plane_sent(0)

            @pl.when(jnp.logical_and(step == planes // 2 + 1, j == 0))
            def _():
                send_plane(planes // 2)

            @pl.when(jnp.logical_and(step == planes // 2 + 1, j == 2))
            def _():
                send_rows(planes // 2)
                plane_sent(planes // 2)

            @pl.when(jnp.logical_and(step > planes // 2 + 1, j == 0))
            def _():
                send_plane(step - 1)
                send_plane(planes - step + 1)

            @pl.when(jnp.logical_and(step > planes // 2 + 1, j == 2))
            def _():
                send_rows(step - 1)
                send_rows(planes - step + 1)
                plane_sent(step - 1)
                plane_sent(planes - step + 1)

        @pl.when(step == 1)
        def _():
            send_pair(0)

        @pl.when(step == planes // 2)
        def _():
            send_pair(planes // 2)

        @pl.when(step > planes // 2)
        def _():
            send_pair(step)
            send_pair(planes - step)

    down_copy(0, half - 1, a_tile(half - 1)).start()

    @pl.loop(0, half - 1)
    def _(j):
        down_copy(last - 1, tiles - 1 - j).wait_recv()
        multiply(1, tiles - 1 - j)

        @pl.when(j > 0)
        def _():
            up_copy(last - 1, j - 1).wait_recv()
            multiply(last, j - 1)

        @pl.when(j == 0)
        def _():
            send_plane(last - 1)
            send_plane(2)

        @pl.when(j == half - 2)
        def _():
            send_pair(1)

    send_direct(1)
    send_rows(last - 1)
    send_rows(2)
    plane_sent(last - 1)
    plane_sent(2)
    for slot in sorted(range(2, last), key=lambda d: abs(planes // 2 - d)):
        row_copy(slot).start()

    up_copy(last - 1, half - 2).wait_recv()
    multiply(last, half - 2)
    down_copy(0, half - 1).wait_recv()
    multiply(last, half - 1)
    send_pair(last)

    send_direct(0)

    @pl.loop(0, half)
    def _(j):
        ring_sent(last - 2, j)

    @pl.loop(0, half - 1)
    def _(j):
        ring_sent(last - 1, j)

    up_copy(0, half).wait_send()
    down_copy(0, half - 1).wait_send()
    pair_copy(1).wait_send()
    pair_copy(last).wait_send()

    take_direct(1)

    @pl.loop(2, last)
    def _(slot):
        take_rows(slot)
        row_copy(slot).wait_send()

    take_direct(0)
    direct_whole(1).wait_send()
    direct_whole(0).wait_send()


def solution(mesh):
    planes, chips = mesh.shape["ab"], mesh.shape["cd"] // 2

    def per_device(amplitudes, integrals, live_tiles, residual_in):
        rows, depth = amplitudes.shape
        tiles, columns = depth // TILE, integrals.shape[1]
        f32, bf16 = jnp.float32, jnp.bfloat16
        dma = pltpu.SemaphoreType.DMA
        ladder = pl.pallas_call(
            functools.partial(kernel, planes, chips, math.isqrt(chips), tiles),
            out_shape=pltpu.VMEM(residual_in.shape, f32),
            in_specs=[
                pl.BlockSpec(memory_space=pltpu.HBM),
                pl.BlockSpec(memory_space=pltpu.HBM),
                pl.BlockSpec(memory_space=pltpu.HBM),
            ],
            out_specs=pl.BlockSpec(memory_space=pltpu.VMEM),
            scratch_shapes=[
                pltpu.VMEM((planes, tiles, rows, TILE), f32),
                pltpu.VMEM((tiles, TILE, columns), f32),
                pltpu.VMEM((tiles, TILE, columns), bf16),
                pltpu.VMEM((tiles, TILE, columns), bf16),
                pltpu.VMEM((planes, 2, rows, HALF), f32),
                pltpu.VMEM((planes, 2, rows, HALF), f32),
                pltpu.VMEM((planes, rows, HALF), f32),
                pltpu.VMEM((planes, (chips - 1) * 8, HALF), f32),
                pltpu.VMEM((planes, 8, HALF), f32),
                pltpu.VMEM((planes, 8, HALF), f32),
                pltpu.VMEM((2, chips * 8, HALF), f32),
                pltpu.SMEM((tiles,), jnp.int32),
                pltpu.SemaphoreType.REGULAR,
                dma(()),
                dma((tiles,)),
                dma((tiles,)),
                dma((planes - 1, tiles)),
                dma((planes - 1, tiles)),
                dma((planes - 1, tiles)),
                dma((planes - 1, tiles)),
                dma((planes,)),
                dma((planes,)),
                dma((planes,)),
                dma((planes,)),
                dma((planes,)),
                dma((planes,)),
                dma((2,)),
                dma((2,)),
            ],
            compiler_params=pltpu.CompilerParams(
                collective_id=0, has_side_effects=True, vmem_limit_bytes=58 * 1024 * 1024
            ),
            cost_estimate=pl.CostEstimate(
                flops=6 * planes * rows * depth * columns,
                bytes_accessed=4 * depth * (rows + columns),
                transcendentals=0,
            ),
        )(amplitudes, integrals, live_tiles)
        return residual_in + ladder

    return jax.shard_map(
        per_device,
        mesh=mesh,
        in_specs=(P("ab", "cd"), P("cd", "ab"), P("cd"), P(("ab", "cd"), None)),
        out_specs=P(("ab", "cd"), None),
        check_vma=False,
    )
```

```python
import functools
import math

import jax
import jax.numpy as jnp
from jax import lax
from jax.experimental import pallas as pl
from jax.experimental.pallas import tpu as pltpu
from jax.sharding import PartitionSpec as P

TILE = 256
HALF = 256
MESH = pl.DeviceIdType.MESH


def kernel(
    planes,
    chips,
    line,
    tiles,
    a_ref,
    b_ref,
    live_ref,
    out_ref,
    a_all,
    b_raw,
    b_hi,
    b_lo,
    part,
    folded,
    pair_recv,
    plane_recv,
    summed,
    land,
    direct,
    live,
    relay,
    live_sem,
    a_sem,
    b_sem,
    up_send,
    up_recv,
    down_send,
    down_recv,
    pair_send,
    pair_got,
    plane_send,
    plane_got,
    row_send,
    row_got,
    direct_send,
    direct_got,
):
    cd = lax.axis_index("cd")
    z = planes - 1 - lax.axis_index("ab")
    chip, core = cd // 2, cd % 2
    twin = cd + 1 - 2 * core
    above, below = (z + 1) % planes, (z + planes - 1) % planes
    half = tiles // 2
    last = planes - 1
    rows = a_ref.shape[0]

    barrier = pltpu.get_barrier_semaphore()

    def greet(cd_at, z_at):
        pl.semaphore_signal(barrier, inc=1, device_id={"cd": cd_at, "ab": planes - 1 - z_at}, device_id_type=MESH)

    greet(cd, above)
    greet(cd, below)
    greet(twin, z)

    across, along = chip // line, chip % line

    def in_row(d):
        return (across * line + (along + d) % line) * 2 + core

    def in_column(d):
        return ((across + d) % line * line + along) * 2 + core

    @pl.loop(1, line)
    def _(d):
        greet(in_row(d), z)
        greet(in_column(d), z)

    def a_tile(t):
        return a_ref.at[:, pl.ds(pl.multiple_of(t * TILE, TILE), TILE)]

    def own_copy(t):
        return pltpu.make_async_copy(a_tile(t), a_all.at[0, t], a_sem.at[t])

    def b_copy(t):
        return pltpu.make_async_copy(
            b_ref.at[pl.ds(pl.multiple_of(t * TILE, TILE), TILE), :], b_raw.at[t], b_sem.at[t]
        )

    pl.semaphore_wait(barrier, 3 + 2 * (line - 1))

    def up_copy(step, t, src=None):
        return pltpu.make_async_remote_copy(
            src_ref=a_all.at[step, t] if src is None else src,
            dst_ref=a_all.at[step + 1, t],
            send_sem=up_send.at[step, t],
            recv_sem=up_recv.at[step, t],
            device_id={"cd": cd, "ab": planes - 1 - above},
            device_id_type=MESH,
        )

    def down_copy(step, t, src=None):
        return pltpu.make_async_remote_copy(
            src_ref=a_all.at[(planes - step) % planes, t] if src is None else src,
            dst_ref=a_all.at[planes - 1 - step, t],
            send_sem=down_send.at[step, t],
            recv_sem=down_recv.at[step, t],
            device_id={"cd": cd, "ab": planes - 1 - below},
            device_id_type=MESH,
        )

    @pl.loop(0, half)
    def _(t):
        up_copy(0, t, a_tile(t)).start()
        down_copy(0, tiles - 1 - t, a_tile(tiles - 1 - t)).start()

    up_copy(0, half, a_tile(half)).start()

    @pl.loop(1, line)
    def _(d):
        pl.semaphore_signal(relay, inc=1, device_id={"cd": in_row(d), "ab": planes - 1 - z}, device_id_type=MESH)

    live_copy = pltpu.make_async_copy(live_ref, live, live_sem)
    live_copy.start()

    @pl.loop(0, tiles)
    def _(t):
        own_copy(t).start()
        b_copy(t).start()

    part[...] = jnp.zeros_like(part)

    live_copy.wait()

    @pl.loop(0, tiles)
    def _(t):
        b_copy(t).wait()
        weight = live[t].astype(jnp.float32)
        whole = b_raw[t] * weight
        high = whole.astype(jnp.bfloat16)
        b_hi[t] = high
        b_lo[t] = (whole - high.astype(jnp.float32)).astype(jnp.bfloat16)

    def multiply(slot, t):
        whole = a_all[slot, t]
        high = whole.astype(jnp.bfloat16)
        low = (whole - high.astype(jnp.float32)).astype(jnp.bfloat16)
        both = jnp.concatenate([high, low], axis=0)
        for h in range(2):
            cols = slice(h * HALF, (h + 1) * HALF)
            first = jnp.dot(both, b_hi[t, :, cols], preferred_element_type=jnp.float32)
            second = jnp.dot(high, b_lo[t, :, cols], preferred_element_type=jnp.float32)
            part[slot, h] += first[:rows] + (first[rows:] + second)

    def pair_copy(slot):
        return pltpu.make_async_remote_copy(
            src_ref=folded.at[slot, 1 - core],
            dst_ref=pair_recv.at[slot],
            send_sem=pair_send.at[slot],
            recv_sem=pair_got.at[slot],
            device_id={"cd": twin, "ab": planes - 1 - z},
            device_id_type=MESH,
        )

    def plane_copy(slot, d):
        to = (chip + d) % chips
        return pltpu.make_async_remote_copy(
            src_ref=folded.at[slot, core, pl.ds(pl.multiple_of(to * 8, 8), 8)],
            dst_ref=plane_recv.at[slot, pl.ds(pl.multiple_of((d - 1) * 8, 8), 8)],
            send_sem=plane_send.at[slot],
            recv_sem=plane_got.at[slot],
            device_id={"cd": to * 2 + core, "ab": planes - 1 - z},
            device_id_type=MESH,
        )

    def plane_whole(slot):
        return pltpu.make_async_remote_copy(
            src_ref=folded.at[slot, core, pl.ds(0, (chips - 1) * 8)],
            dst_ref=plane_recv.at[slot],
            send_sem=plane_send.at[slot],
            recv_sem=plane_got.at[slot],
            device_id={"cd": twin, "ab": planes - 1 - z},
            device_id_type=MESH,
        )

    def row_copy(slot):
        return pltpu.make_async_remote_copy(
            src_ref=summed.at[slot],
            dst_ref=land.at[slot],
            send_sem=row_send.at[slot],
            recv_sem=row_got.at[slot],
            device_id={"cd": cd, "ab": planes - 1 - (z + planes - slot) % planes},
            device_id_type=MESH,
        )

    away = sorted(
        ((dx, dy) for dx in range(line) for dy in range(line)),
        key=lambda d: -min(d[0], line - d[0]) - min(d[1], line - d[1]),
    )

    def direct_copy(way, at):
        dx, dy = away[at]
        to = (across + dx) % line * line + (along + dy) % line
        return pltpu.make_async_remote_copy(
            src_ref=folded.at[(last, 1)[way], core, pl.ds(pl.multiple_of(to * 8, 8), 8)],
            dst_ref=direct.at[way, pl.ds(at * 8, 8)],
            send_sem=direct_send.at[way],
            recv_sem=direct_got.at[way],
            device_id={"cd": to * 2 + core, "ab": planes - 1 - (above, below)[way]},
            device_id_type=MESH,
        )

    def direct_whole(way):
        return pltpu.make_async_remote_copy(
            src_ref=folded.at[(last, 1)[way], core],
            dst_ref=direct.at[way],
            send_sem=direct_send.at[way],
            recv_sem=direct_got.at[way],
            device_id={"cd": cd, "ab": planes - 1 - (above, below)[way]},
            device_id_type=MESH,
        )

    def send_direct(way):
        slot = (last, 1)[way]
        pair_copy(slot).wait_recv()
        folded[slot, core] += pair_recv[slot]
        for at in range(chips):
            direct_copy(way, at).start()

    def take_direct(way):
        direct_whole(way).wait_recv()
        write_rows((last, 1)[way], jnp.sum(direct[way].reshape(chips, 8, HALF), axis=0))

    def send_pair(slot):
        left, right = part[slot, 0], part[slot, 1]
        upper = lax.broadcasted_iota(jnp.int32, left.shape, 0) % 8 < 4
        folded[slot, 0] = jnp.where(upper, left, pltpu.roll(right, 4, 0))
        folded[slot, 1] = jnp.where(upper, pltpu.roll(left, rows - 4, 0), right)
        pair_copy(slot).start()

    def send_plane(slot):
        pair_copy(slot).wait_recv()
        folded[slot, core] += pair_recv[slot]

        @pl.loop(1, chips)
        def _(d):
            plane_copy(slot, d).start()

    def write_rows(slot, got):
        first = (planes - 1 - (z + slot) % planes) * (2 * HALF)
        for h in range(2):
            cols = pl.ds(pl.multiple_of(first + h * HALF, HALF), HALF)
            out_ref[:, cols] = got[4 * h : 4 * h + 4]

    def send_rows(slot):
        plane_whole(slot).wait_recv()
        mine = folded[slot, core, pl.ds(pl.multiple_of(chip * 8, 8), 8)]
        total = mine + jnp.sum(plane_recv[slot].reshape(chips - 1, 8, HALF), axis=0)
        if isinstance(slot, int) and slot == 0:
            write_rows(0, total)
        else:
            summed[slot] = total

    def take_rows(slot):
        row_copy(slot).wait_recv()
        write_rows(slot, land[slot])

    @pl.loop(0, tiles)
    def _(t):
        own_copy(t).wait()

    def forward_up(step, j):
        up_copy(step - 1, j).wait_recv()

        @pl.when(jnp.logical_or(step < last - 1, jnp.logical_and(step < last, j < half - 1)))
        def _():
            up_copy(step, j).start()

    def forward_down(step, j):
        down_copy(step - 1, tiles - 1 - j).wait_recv()

        @pl.when(jnp.logical_or(step < last - 1, jnp.logical_and(step < last, j < half - 1)))
        def _():
            down_copy(step, tiles - 1 - j).start()

    def ring_sent(step, j):
        up_copy(step, j).wait_send()
        down_copy(step, tiles - 1 - j).wait_send()

    def plane_sent(slot):
        pair_copy(slot).wait_send()
        plane_whole(slot).wait_send()

    @pl.loop(1, last)
    def _(step):
        @pl.loop(0, half)
        def _(j):
            forward_up(step, j)
            forward_down(step, j)
            multiply(step, j)
            multiply(planes - step, tiles - 1 - j)

            @pl.when(step == 1)
            def _():
                multiply(0, j)
                multiply(0, tiles - 1 - j)

            @pl.when(step > 1)
            def _():
                ring_sent(step - 2, j)

            @pl.when(jnp.logical_and(step == 1, j == 2))
            def _():
                up_copy(0, half).wait_recv()
                multiply(1, half)

            @pl.when(jnp.logical_and(step == 2, j == 0))
            def _():
                pl.semaphore_wait(relay, line - 1)
                send_plane(0)

            @pl.when(jnp.logical_and(step == 2, j == 2))
            def _():
                send_rows(0)
                plane_sent(0)

            @pl.when(jnp.logical_and(step == planes // 2 + 1, j == 0))
            def _():
                send_plane(planes // 2)

            @pl.when(jnp.logical_and(step == planes // 2 + 1, j == 2))
            def _():
                send_rows(planes // 2)
                plane_sent(planes // 2)

            @pl.when(jnp.logical_and(step > planes // 2 + 1, j == 0))
            def _():
                send_plane(step - 1)
                send_plane(planes - step + 1)

            @pl.when(jnp.logical_and(step > planes // 2 + 1, j == 2))
            def _():
                send_rows(step - 1)
                send_rows(planes - step + 1)
                plane_sent(step - 1)
                plane_sent(planes - step + 1)

        @pl.when(step == 1)
        def _():
            send_pair(0)

        @pl.when(step == planes // 2)
        def _():
            send_pair(planes // 2)

        @pl.when(step > planes // 2)
        def _():
            send_pair(step)
            send_pair(planes - step)

    down_copy(0, half - 1, a_tile(half - 1)).start()

    @pl.loop(0, half - 1)
    def _(j):
        down_copy(last - 1, tiles - 1 - j).wait_recv()
        multiply(1, tiles - 1 - j)

        @pl.when(j == half - 2)
        def _():
            send_pair(1)

        @pl.when(j > 0)
        def _():
            up_copy(last - 1, j - 1).wait_recv()
            multiply(last, j - 1)

        @pl.when(j == 0)
        def _():
            send_plane(last - 1)
            send_plane(2)

    send_direct(1)
    send_rows(last - 1)
    send_rows(2)
    plane_sent(last - 1)
    plane_sent(2)
    for slot in sorted(range(2, last), key=lambda d: abs(planes // 2 - d)):
        row_copy(slot).start()

    up_copy(last - 1, half - 2).wait_recv()
    multiply(last, half - 2)
    down_copy(0, half - 1).wait_recv()
    multiply(last, half - 1)
    send_pair(last)

    send_direct(0)

    @pl.loop(0, half)
    def _(j):
        ring_sent(last - 2, j)

    @pl.loop(0, half - 1)
    def _(j):
        ring_sent(last - 1, j)

    up_copy(0, half).wait_send()
    down_copy(0, half - 1).wait_send()
    pair_copy(1).wait_send()
    pair_copy(last).wait_send()

    take_direct(1)

    @pl.loop(2, last)
    def _(slot):
        take_rows(slot)
        row_copy(slot).wait_send()

    take_direct(0)
    direct_whole(1).wait_send()
    direct_whole(0).wait_send()


def solution(mesh):
    planes, chips = mesh.shape["ab"], mesh.shape["cd"] // 2

    def per_device(amplitudes, integrals, live_tiles, residual_in):
        rows, depth = amplitudes.shape
        tiles, columns = depth // TILE, integrals.shape[1]
        f32, bf16 = jnp.float32, jnp.bfloat16
        dma = pltpu.SemaphoreType.DMA
        ladder = pl.pallas_call(
            functools.partial(kernel, planes, chips, math.isqrt(chips), tiles),
            out_shape=pltpu.VMEM(residual_in.shape, f32),
            in_specs=[
                pl.BlockSpec(memory_space=pltpu.HBM),
                pl.BlockSpec(memory_space=pltpu.HBM),
                pl.BlockSpec(memory_space=pltpu.HBM),
            ],
            out_specs=pl.BlockSpec(memory_space=pltpu.VMEM),
            scratch_shapes=[
                pltpu.VMEM((planes, tiles, rows, TILE), f32),
                pltpu.VMEM((tiles, TILE, columns), f32),
                pltpu.VMEM((tiles, TILE, columns), bf16),
                pltpu.VMEM((tiles, TILE, columns), bf16),
                pltpu.VMEM((planes, 2, rows, HALF), f32),
                pltpu.VMEM((planes, 2, rows, HALF), f32),
                pltpu.VMEM((planes, rows, HALF), f32),
                pltpu.VMEM((planes, (chips - 1) * 8, HALF), f32),
                pltpu.VMEM((planes, 8, HALF), f32),
                pltpu.VMEM((planes, 8, HALF), f32),
                pltpu.VMEM((2, chips * 8, HALF), f32),
                pltpu.SMEM((tiles,), jnp.int32),
                pltpu.SemaphoreType.REGULAR,
                dma(()),
                dma((tiles,)),
                dma((tiles,)),
                dma((planes - 1, tiles)),
                dma((planes - 1, tiles)),
                dma((planes - 1, tiles)),
                dma((planes - 1, tiles)),
                dma((planes,)),
                dma((planes,)),
                dma((planes,)),
                dma((planes,)),
                dma((planes,)),
                dma((planes,)),
                dma((2,)),
                dma((2,)),
            ],
            compiler_params=pltpu.CompilerParams(
                collective_id=0, has_side_effects=True, vmem_limit_bytes=58 * 1024 * 1024
            ),
            cost_estimate=pl.CostEstimate(
                flops=6 * planes * rows * depth * columns,
                bytes_accessed=4 * depth * (rows + columns),
                transcendentals=0,
            ),
        )(amplitudes, integrals, live_tiles)
        return residual_in + ladder

    return jax.shard_map(
        per_device,
        mesh=mesh,
        in_specs=(P("ab", "cd"), P("cd", "ab"), P("cd"), P(("ab", "cd"), None)),
        out_specs=P(("ab", "cd"), None),
        check_vma=False,
    )
```
